32 devices in a mesh: seg: 4 (over y, x), op: 8 (over z, core).
Axes of the slice: x: 2, y: 2, z: 4, core: 2. Of those that a mesh axis runs over, the one named last changes fastest.
Arguments:
- theta: bfloat16 [4, 8, 512, 512], P('seg', 'op'), may hold values from -21 to 21
- left_edge: bfloat16 [8, 512, 512], P('op'), may hold values from -1 to 4
- transfer: bfloat16 [4, 8, 512, 512], P('seg', 'op'), may hold values from -1 to 2
- right_env: bfloat16 [4, 8, 512, 512], P('seg', 'op'), may hold values from -1 to 4
- coupling: bfloat16 [4, 8, 512, 512], P('seg', 'op'), may hold values from -0.25 to 0.25
- left_sizes: int32 [8], P('op'), may hold values from 1 to 512, 3072 in all
- right_sizes: int32 [8], P('op'), may hold values from 1 to 512, 3072 in all
Outputs:
- theta_out: float32 [4, 8, 512, 512], P('seg', 'op')
- left_env: bfloat16 [4, 8, 512, 512], P('seg', 'op')
- energy: float32 [4], P('seg')
- first_energy: float32 [4], P('seg')
The draws below stay inside these ranges and needn't reach their ends.
All inputs are finite; a program needn't handle non-finite values. No bound on the sum of `left_sizes` or of `right_sizes` on one device may be relied on, other than what follows from the above.
Results may differ from the reference program's by a relative error of at most 0.0085.
Values may be sent and summed in bfloat16 or wider, within the bound.
A program may use at most 128 MiB of HBM per device.

```python
import math
import jax
import jax.numpy as jnp
import numpy as np
from jax import lax

BLK = 512
DAVIDSON = 4
SECTORS = 8
SEGMENTS = 4


def scaled_noise(key, shape):
    noise = jnp.clip(jax.random.normal(key, shape, jnp.float32), -4.0, 4.0)
    return noise / jnp.sqrt(jnp.float32(BLK))


def draw_transfer(key, part):
    shape = (SEGMENTS, SECTORS, BLK, BLK)
    noise = scaled_noise(jax.random.fold_in(key, 11), shape)
    identity = jnp.eye(BLK, dtype=jnp.float32)
    return (identity + 0.25 * noise).astype(jnp.bfloat16)


def draw_left_edge(key, part):
    shape = (SECTORS, BLK, BLK)
    noise = scaled_noise(jax.random.fold_in(key, 23), shape)
    level = jax.random.uniform(jax.random.fold_in(key, 29), (SECTORS,), jnp.float32, 0.5, 1.5)
    identity = jnp.eye(BLK, dtype=jnp.float32)
    return (identity[None] * level[:, None, None] + noise).astype(jnp.bfloat16)


def draw_right_env(key, part):
    shape = (SEGMENTS, SECTORS, BLK, BLK)
    noise = scaled_noise(jax.random.fold_in(key, 37), shape)
    log_level = jax.random.uniform(jax.random.fold_in(key, 41), (SEGMENTS,), jnp.float32, jnp.log(0.5), jnp.log(2.0))
    sector_level = jax.random.uniform(jax.random.fold_in(key, 43), (SEGMENTS, SECTORS), jnp.float32, 0.75, 1.25)
    level = jnp.exp(log_level)[:, None] * sector_level
    identity = jnp.eye(BLK, dtype=jnp.float32)
    return (identity[None, None] * level[:, :, None, None] + noise).astype(jnp.bfloat16)


def draw_theta(key, part):
    shape = (SEGMENTS, SECTORS, BLK, BLK)
    subkey = jax.random.fold_in(key, 53)
    position = jnp.arange(SECTORS, dtype=jnp.float32) / jnp.float32(SECTORS - 1)
    noise = jnp.clip(jax.random.normal(subkey, shape, jnp.float32), -4.0, 4.0)
    level = jnp.exp(jnp.log(5.0) * position)
    return (noise * level[None, :, None, None]).astype(jnp.bfloat16)


def levels(stream_key, dims, shards, least, top_value):
    factor_of, own = 1.0, jax.random.fold_in(stream_key, 6)
    for dim, blocks in shards:
        draws = jnp.exp(jax.random.uniform(jax.random.fold_in(own, dim), (blocks,), jnp.float32, least / len(shards), top_value / len(shards)))
        factor_of = factor_of * jnp.repeat(draws, dims[dim] // blocks).reshape([-1 if axis == dim else 1 for axis in range(len(dims))])
    return factor_of


def length_profile(amount, total, bound, slope):
    weights = [(1 << 20) // math.isqrt(grade ** slope) + 1 for grade in range(2, amount + 1)]
    rest, holding = total - bound - (amount - 1), [1] * (amount - 1)
    while rest > 0:
        movable = [i for i in range(amount - 1) if holding[i] < bound]
        whole, left = sum([weights[i] for i in movable]), rest
        for i in movable:
            more = min(bound - holding[i], max(1, left * weights[i] // whole), rest)
            holding[i] = holding[i] + more
            rest = rest - more
    return np.array([bound] + holding)


def ragged(own_key, amount, total, most, lean):
    if amount == 2:
        one = jax.random.randint(own_key, (), max(1, total - most), min(most, total - 1) + 1)
        return jnp.stack([one, total - one])
    tallies = jnp.asarray(length_profile(amount, total, most, lean), jnp.int32)
    couples = (amount - 1) // 2
    giver, receiver = tallies[1:1 + 2 * couples:2], tallies[2:2 + 2 * couples:2]
    room = jnp.minimum(giver - 1, most - receiver)
    passed = jax.random.randint(jax.random.fold_in(own_key, 1), (couples,), 0, 1 << 20) % (room + 1)
    tallies = tallies.at[1:1 + 2 * couples:2].set(giver - passed).at[2:2 + 2 * couples:2].set(receiver + passed)
    return tallies[jax.random.permutation(jax.random.fold_in(own_key, 2), amount)]


def bell_draw(stream_key, shape, scale, most, cuts=(), kind=jnp.bfloat16):
    values = jax.random.normal(stream_key, shape, jnp.float32) * scale
    if len(cuts) > 0:
        values = levels(stream_key, shape, cuts, -0.22, 0.18) * values
    return jnp.clip(values, min=-most, max=most).astype(kind)


def setup_inputs(seed: int = 0) -> dict:
    key_list = jax.random.split(jax.random.key(seed), 8)
    return {
        "theta": draw_theta(jax.random.fold_in(key_list[7], 71), 0),
        "left_edge": draw_left_edge(jax.random.fold_in(key_list[7], 71), 0),
        "transfer": draw_transfer(jax.random.fold_in(key_list[7], 71), 0),
        "right_env": draw_right_env(jax.random.fold_in(key_list[7], 71), 0),
        "coupling": bell_draw(key_list[4], (SEGMENTS, SECTORS, BLK, BLK), BLK ** -0.5, 0.25, ((0, 4), (1, 8))),
        "left_sizes": ragged(key_list[5], SECTORS, SECTORS * BLK * 3 // 4, BLK, 1).astype(jnp.int32),
        "right_sizes": ragged(key_list[6], SECTORS, SECTORS * BLK * 3 // 4, BLK, 1).astype(jnp.int32),
    }


epsilon = 1e-06

def symmetric(block):
    return 0.5 * (block + jnp.swapaxes(block, -1, -2))

def apply_all(field, left_block, right_block, coupling_blk, live_mask):
    field_wide = field.astype(jnp.float32)
    middle = jnp.einsum('kij,kjl->kil', left_block.astype(jnp.float32), field_wide).astype(jnp.bfloat16)
    diagonal_term = jnp.einsum('kij,kjl->kil', middle.astype(jnp.float32), right_block.astype(jnp.float32))
    coupling_wide = coupling_blk.astype(jnp.float32)
    previous = jnp.concatenate([jnp.zeros_like(field_wide[:1]), field_wide[:-1]], 0)
    lower_term = jnp.einsum('kij,kjl->kil', coupling_wide, previous)
    lifted = jnp.einsum('kji,kjl->kil', coupling_wide, field_wide)
    upper_part = jnp.concatenate([lifted[1:], jnp.zeros_like(lifted[:1])], 0)
    return live_mask * (diagonal_term + lower_term + upper_part)

def reference(theta, left_edge, transfer, right_env, coupling, left_sizes, right_sizes):
    row_index = lax.broadcasted_iota(jnp.int32, (SECTORS, BLK, BLK), 1)
    col_index = lax.broadcasted_iota(jnp.int32, (SECTORS, BLK, BLK), 2)
    live_mask = ((row_index < left_sizes[:, None, None]) & (col_index < right_sizes[:, None, None])).astype(jnp.float32)
    edge_sym = symmetric(left_edge.astype(jnp.float32))
    identity = jnp.broadcast_to(jnp.eye(BLK, dtype=jnp.float32), (SECTORS, BLK, BLK))
    highest = lax.Precision.HIGHEST

    def segment_solve(prefix, pieces):
        start_blk, step_blk, right_raw, coupling_blk = pieces
        left_block = jnp.einsum('kji,kjl->kil', prefix, edge_sym, precision=highest)
        left_block = jnp.einsum('kij,kjl->kil', left_block, prefix, precision=highest).astype(jnp.bfloat16)
        right_block = symmetric(right_raw.astype(jnp.float32)).astype(jnp.bfloat16)
        start = live_mask * start_blk.astype(jnp.float32)
        vector = start / jnp.sqrt(jnp.sum(start * start) + epsilon)
        image = apply_all(vector.astype(jnp.bfloat16), left_block, right_block, coupling_blk, live_mask)
        energy = jnp.sum(vector * image)
        first_value = energy
        for sweep_step in range(DAVIDSON):
            residual = image - energy * vector
            correction = residual.astype(jnp.bfloat16)
            corr_wide = correction.astype(jnp.float32)
            applied = apply_all(correction, left_block, right_block, coupling_blk, live_mask)
            corr_norm = jnp.sum(corr_wide * corr_wide)
            cross_term = jnp.sum(image * corr_wide)
            curv_term = jnp.sum(corr_wide * applied)
            scale_norm = jnp.sqrt(corr_norm + epsilon)
            offdiag = cross_term / scale_norm
            diag_value = curv_term / (corr_norm + epsilon)
            half_gap = (diag_value - energy) / 2
            lowest = (energy + diag_value) / 2 - jnp.sqrt(half_gap * half_gap + offdiag * offdiag)
            rotation = lowest - energy
            radius = jnp.sqrt(offdiag * offdiag + rotation * rotation + epsilon)
            vector = (offdiag * vector + rotation * corr_wide / scale_norm) / radius
            image = (offdiag * image + rotation * applied / scale_norm) / radius
            energy = lowest
        prefix_next = jnp.einsum('kij,kjl->kil', prefix, step_blk.astype(jnp.float32), precision=highest)
        return (prefix_next, (vector, left_block, energy, first_value))
    final_prefix, outputs = lax.scan(segment_solve, identity, (theta, transfer, right_env, coupling))
    return (outputs[0], outputs[1], outputs[2], outputs[3])
```

```python
import functools

import jax
import jax.numpy as jnp
from jax import lax
from jax.experimental import pallas as pl
from jax.experimental.pallas import tpu as pltpu
from jax.sharding import PartitionSpec as P

DAVIDSON = 4
STEPS = DAVIDSON + 1
ROUNDS = DAVIDSON + 2
CHUNKS = 2

epsilon = 1e-06

MESH = pl.DeviceIdType.MESH
f32 = jnp.float32
bf16 = jnp.bfloat16


def mm(a, b):
    return jnp.dot(a, b, preferred_element_type=f32)


def split(x):
    high = x.astype(bf16)
    return high, (x - high.astype(f32)).astype(bf16)


def folded(x):
    rows, width = x.shape
    x = jnp.sum(x.reshape(rows // 8, 8, width), axis=0)
    acc = x[:, :128]
    for start in range(128, width, 128):
        acc = acc + x[:, start : start + 128]
    return jnp.sum(acc, axis=0, keepdims=True)


def kernel(
    n_seg, n_op,
    theta_ref, edge_ref, transfer_ref, right_ref, coupling_ref, rows_ref, cols_ref,
    vec_out, left_out, energy_out, first_out,
    field, prev, foll, next_coupling, lifted_coupling, arrived, left_wide, right_blk, middle,
    vec, img, app, sums, level,
    field_send, prev_recv, foll_recv, t_send, t_recv, c_send, c_recv, sum_send, sum_recv,
):
    seg = lax.axis_index("seg")
    me = lax.axis_index("op")
    size = theta_ref.shape[-1]
    width = size // CHUNKS
    has_prev = me > 0
    has_next = me < n_op - 1

    barrier = pltpu.get_barrier_semaphore()
    for d in range(1, n_seg):
        pl.semaphore_signal(
            barrier, inc=1, device_id=(lax.rem(seg + d, n_seg), me), device_id_type=MESH
        )
    for d in range(1, n_op):
        pl.semaphore_signal(
            barrier, inc=1, device_id=(seg, lax.rem(me + d, n_op)), device_id_type=MESH
        )

    live_rows = lax.broadcasted_iota(jnp.int32, (size, width), 0) < rows_ref[0]

    def live(c):
        cols = lax.broadcasted_iota(jnp.int32, (size, width), 1) + c * width
        return live_rows & (cols < cols_ref[0])

    for c in range(CHUNKS):
        cs = pl.ds(c * width, width)
        field[0, c] = jnp.where(live(c), theta_ref[0, 0, :, cs].astype(f32), 0.0).astype(bf16)

    pl.semaphore_wait(barrier, n_seg + n_op - 2)

    def t_copy(d):
        return pltpu.make_async_remote_copy(
            src_ref=transfer_ref.at[0, 0], dst_ref=arrived.at[seg],
            send_sem=t_send.at[d], recv_sem=t_recv.at[seg],
            device_id=(seg + d, me), device_id_type=MESH,
        )

    for d in range(1, n_seg):
        @pl.when(seg + d < n_seg)
        def _():
            t_copy(d).start()

    def up_copy(step, c):
        return pltpu.make_async_remote_copy(
            src_ref=field.at[step, c], dst_ref=prev.at[step, c],
            send_sem=field_send.at[step, 0, c], recv_sem=prev_recv.at[step, c],
            device_id=(seg, me + 1), device_id_type=MESH,
        )

    def down_copy(step, c):
        return pltpu.make_async_remote_copy(
            src_ref=field.at[step, c], dst_ref=foll.at[step, c],
            send_sem=field_send.at[step, 1, c], recv_sem=foll_recv.at[step, c],
            device_id=(seg, me - 1), device_id_type=MESH,
        )

    def send_field(step, c):
        @pl.when(has_next)
        def _():
            up_copy(step, c).start()

        @pl.when(has_prev)
        def _():
            down_copy(step, c).start()

    def take_field(step, c):
        @pl.when(has_prev)
        def _():
            up_copy(step, c).wait_recv()

        @pl.when(has_next)
        def _():
            down_copy(step, c).wait_recv()

    def settle_field(step, c):
        @pl.when(has_next)
        def _():
            up_copy(step, c).wait_send()

        @pl.when(has_prev)
        def _():
            down_copy(step, c).wait_send()

    def coupling_copy():
        return pltpu.make_async_remote_copy(
            src_ref=coupling_ref.at[0, 0], dst_ref=next_coupling,
            send_sem=c_send, recv_sem=c_recv,
            device_id=(seg, me - 1), device_id_type=MESH,
        )

    for c in range(CHUNKS):
        send_field(0, c)

    @pl.when(has_prev)
    def _():
        coupling_copy().start()

    def sum_copy(rnd, d):
        return pltpu.make_async_remote_copy(
            src_ref=sums.at[rnd, me], dst_ref=sums.at[rnd, me],
            send_sem=sum_send.at[rnd, d], recv_sem=sum_recv.at[rnd, me],
            device_id=(seg, lax.rem(me + d, n_op)), device_id_type=MESH,
        )

    def sum_start(rnd, parts):
        row = lax.broadcasted_iota(jnp.int32, (8, 128), 0)
        tile = jnp.zeros((8, 128), f32)
        for i, part in enumerate(parts):
            tile = jnp.where(row == i, part, tile)
        sums[rnd, me] = tile
        for d in range(1, n_op):
            sum_copy(rnd, d).start()

    def sum_finish(rnd, count):
        for d in range(1, n_op):
            source = lax.rem(me + d, n_op)
            pltpu.make_async_remote_copy(
                src_ref=sums.at[rnd, source], dst_ref=sums.at[rnd, source],
                send_sem=sum_send.at[rnd, d], recv_sem=sum_recv.at[rnd, source],
                device_id=(seg, source), device_id_type=MESH,
            ).wait_recv()
        total = sums[rnd, 0]
        for p in range(1, n_op):
            total = total + sums[rnd, p]
        total = jnp.sum(total, axis=1, keepdims=True)
        return [total[i : i + 1] for i in range(count)]

    def sum_settle(rnd):
        for d in range(1, n_op):
            sum_copy(rnd, d).wait_send()

    start_part = jnp.zeros((1, 128), f32)
    for c in range(CHUNKS):
        wide = field[0, c].astype(f32)
        start_part += folded(wide * wide)
    sum_start(0, [start_part])

    right = right_ref[0, 0].astype(f32)
    right_blk[...] = (0.5 * (right + right.T)).astype(bf16)

    @pl.when(jnp.logical_not(has_prev))
    def _():
        prev[...] = jnp.zeros_like(prev)

    @pl.when(jnp.logical_not(has_next))
    def _():
        foll[...] = jnp.zeros_like(foll)
        lifted_coupling[...] = jnp.zeros_like(lifted_coupling)

    edge = edge_ref[0].astype(f32)
    left_wide[...] = 0.5 * (edge + edge.T)

    (start_total,) = sum_finish(0, 1)
    start_norm = jnp.sqrt(start_total + epsilon)

    @pl.when(has_next)
    def _():
        down = coupling_copy()
        down.wait_recv()
        lifted_coupling[...] = next_coupling[...].astype(f32).T.astype(bf16)

    for c in range(CHUNKS):
        vec[c] = field[0, c].astype(f32) / start_norm
        take_field(0, c)
        before = (prev[0, c].astype(f32) / start_norm).astype(bf16)
        after = (foll[0, c].astype(f32) / start_norm).astype(bf16)
        app[c] = mm(coupling_ref[0, 0], before) + mm(lifted_coupling[...], after)

    for j in range(n_seg - 1):
        @pl.when(j < seg)
        def _():
            pltpu.make_async_remote_copy(
                src_ref=transfer_ref.at[0, 0], dst_ref=arrived.at[j],
                send_sem=t_send.at[0], recv_sem=t_recv.at[j],
                device_id=(seg - 1, me), device_id_type=MESH,
            ).wait_recv()
            step = arrived[j]
            flipped = step.astype(f32).T.astype(bf16)
            high, low = split(left_wide[...])
            high, low = split(mm(high, step) + mm(low, step))
            left_wide[...] = mm(flipped, high) + mm(flipped, low)

    left_out[0, 0] = left_wide[...].astype(bf16)

    for c in range(CHUNKS):
        cs = pl.ds(c * width, width)
        middle[:, cs] = mm(left_out[0, 0], vec[c].astype(bf16)).astype(bf16)
    energy_part = jnp.zeros((1, 128), f32)
    for c in range(CHUNKS):
        cs = pl.ds(c * width, width)
        image = jnp.where(live(c), mm(middle[...], right_blk[:, cs]) + app[c], 0.0)
        img[c] = image
        energy_part += folded(vec[c] * image)
    sum_start(1, [energy_part])
    (energy,) = sum_finish(1, 1)
    first_out[0] = energy[0, 0]

    for c in range(CHUNKS):
        field[1, c] = (img[c] - energy * vec[c]).astype(bf16)
        send_field(1, c)
    level[...] = jnp.broadcast_to(energy, level.shape)

    def sweep(step, carry):
        energy = level[0:1, 0:1]
        norm_part = jnp.zeros((1, 128), f32)
        cross_part = jnp.zeros((1, 128), f32)
        curv_part = jnp.zeros((1, 128), f32)
        for c in range(CHUNKS):
            cs = pl.ds(c * width, width)
            middle[:, cs] = mm(left_out[0, 0], field[step, c]).astype(bf16)
        for c in range(CHUNKS):
            cs = pl.ds(c * width, width)
            app[c] = mm(middle[...], right_blk[:, cs])
            wide = field[step, c].astype(f32)
            norm_part += folded(wide * wide)
            cross_part += folded(img[c] * wide)
        for c in range(CHUNKS):
            take_field(step, c)
            applied = app[c] + mm(coupling_ref[0, 0], prev[step, c])
            applied = applied + mm(lifted_coupling[...], foll[step, c])
            applied = jnp.where(live(c), applied, 0.0)
            app[c] = applied
            curv_part += folded(applied * field[step, c].astype(f32))
        sum_start(step + 1, [norm_part, cross_part, curv_part])
        corr_norm, cross_term, curv_term = sum_finish(step + 1, 3)

        scale_norm = jnp.sqrt(corr_norm + epsilon)
        offdiag = cross_term / scale_norm
        diag_value = curv_term / (corr_norm + epsilon)
        half_gap = (diag_value - energy) / 2
        lowest = (energy + diag_value) / 2 - jnp.sqrt(half_gap * half_gap + offdiag * offdiag)
        rotation = lowest - energy
        radius = jnp.sqrt(offdiag * offdiag + rotation * rotation + epsilon)
        keep = offdiag / radius
        turn = rotation / scale_norm / radius
        level[...] = jnp.broadcast_to(lowest, level.shape)

        @pl.when(step < DAVIDSON)
        def _():
            for c in range(CHUNKS):
                vector = keep * vec[c] + turn * field[step, c].astype(f32)
                image = keep * img[c] + turn * app[c]
                field[step + 1, c] = (image - lowest * vector).astype(bf16)
                send_field(step + 1, c)
                vec[c] = vector
                img[c] = image

        @pl.when(step == DAVIDSON)
        def _():
            for c in range(CHUNKS):
                cs = pl.ds(c * width, width)
                vec_out[0, 0, :, cs] = keep * vec[c] + turn * field[step, c].astype(f32)

        for c in range(CHUNKS):
            settle_field(step, c)
        sum_settle(step + 1)
        return carry

    lax.fori_loop(1, STEPS, sweep, 0)
    energy_out[0] = level[0:1, 0:1][0, 0]

    for d in range(1, n_seg):
        @pl.when(seg + d < n_seg)
        def _():
            t_copy(d).wait_send()
    for c in range(CHUNKS):
        settle_field(0, c)

    @pl.when(has_prev)
    def _():
        coupling_copy().wait_send()

    sum_settle(0)
    sum_settle(1)


def on_device(n_seg, n_op, *arrays):
    size = arrays[0].shape[-1]
    width = size // CHUNKS
    vmem = pl.BlockSpec(memory_space=pltpu.VMEM)
    smem = pl.BlockSpec(memory_space=pltpu.SMEM)
    dma = pltpu.SemaphoreType.DMA
    fields = (STEPS, CHUNKS, size, width)
    return pl.pallas_call(
        functools.partial(kernel, n_seg, n_op),
        out_shape=(
            jax.ShapeDtypeStruct((1, 1, size, size), f32),
            jax.ShapeDtypeStruct((1, 1, size, size), bf16),
            jax.ShapeDtypeStruct((1,), f32),
            jax.ShapeDtypeStruct((1,), f32),
        ),
        in_specs=[vmem] * 5 + [smem] * 2,
        out_specs=(vmem, vmem, smem, smem),
        scratch_shapes=[
            pltpu.VMEM(fields, bf16),
            pltpu.VMEM(fields, bf16),
            pltpu.VMEM(fields, bf16),
            pltpu.VMEM((size, size), bf16),
            pltpu.VMEM((size, size), bf16),
            pltpu.VMEM((n_seg - 1, size, size), bf16),
            pltpu.VMEM((size, size), f32),
            pltpu.VMEM((size, size), bf16),
            pltpu.VMEM((size, size), bf16),
            pltpu.VMEM((CHUNKS, size, width), f32),
            pltpu.VMEM((CHUNKS, size, width), f32),
            pltpu.VMEM((CHUNKS, size, width), f32),
            pltpu.VMEM((ROUNDS, n_op, 8, 128), f32),
            pltpu.VMEM((8, 128), f32),
            dma((STEPS, 2, CHUNKS)),
            dma((STEPS, CHUNKS)),
            dma((STEPS, CHUNKS)),
            dma((n_seg,)),
            dma((n_seg,)),
            dma,
            dma,
            dma((ROUNDS, n_op)),
            dma((ROUNDS, n_op)),
        ],
        compiler_params=pltpu.CompilerParams(
            collective_id=0, has_side_effects=True, vmem_limit_bytes=48 * 1024 * 1024
        ),
        cost_estimate=pl.CostEstimate(
            flops=2 * 30 * size**3, bytes_accessed=8 * size * size * 2, transcendentals=0
        ),
        name="segment_solve",
    )(*arrays)


def solution(mesh):
    placed = (
        P("seg", "op", None, None),
        P("op", None, None),
        P("seg", "op", None, None),
        P("seg", "op", None, None),
        P("seg", "op", None, None),
        P("op"),
        P("op"),
    )
    return jax.shard_map(
        functools.partial(on_device, mesh.shape["seg"], mesh.shape["op"]),
        mesh=mesh,
        in_specs=placed,
        out_specs=(P("seg", "op", None, None), P("seg", "op", None, None), P("seg"), P("seg")),
        check_vma=False,
    )
```

```python
import functools

import jax
import jax.numpy as jnp
from jax import lax
from jax.experimental import pallas as pl
from jax.experimental.pallas import tpu as pltpu
from jax.sharding import PartitionSpec as P

DAVIDSON = 4
STEPS = DAVIDSON + 2
ROUNDS = DAVIDSON + 2
CHUNKS = 2
ROW_BLOCKS = 16
VMEM_LIMIT = 63 * 1024 * 1024

epsilon = 1e-06

MESH = pl.DeviceIdType.MESH
f32 = jnp.float32
bf16 = jnp.bfloat16


def mm(a, b):
    return jnp.dot(a, b, preferred_element_type=f32)


def split(x):
    high = x.astype(bf16)
    return high, (x - high.astype(f32)).astype(bf16)


def folded8(x):
    rows, width = x.shape
    x = jnp.sum(x.reshape(rows // 8, 8, width), axis=0)
    acc = x[:, :128]
    for start in range(128, width, 128):
        acc = acc + x[:, start : start + 128]
    return acc


def folded(x):
    return jnp.sum(folded8(x), axis=0, keepdims=True)


def kernel(
    n_seg, n_op,
    theta_ref, edge_ref, transfer_ref, right_ref, coupling_ref, rows_ref, cols_ref,
    vec_out, left_out, energy_out, first_out,
    theta, edge, right, coupling, own_step, first_left, flipped,
    field, prev, foll, next_coupling, lifted_coupling, arrived, left_wide, right_blk,
    middle, middle_low, low, vec, img, him, app, sums, level,
    load_sem, l_send, l_recv, field_send, prev_recv, foll_recv, t_send, t_recv, c_send, c_recv, sum_send, sum_recv,
):
    seg = lax.axis_index("seg")
    me = lax.axis_index("op")
    size = theta_ref.shape[-1]
    width = size // CHUNKS
    square = n_seg == 4
    has_prev = me > 0
    has_next = me < n_op - 1

    loads = [
        pltpu.make_async_copy(ref, held, load_sem.at[i])
        for i, (ref, held) in enumerate((
            (theta_ref.at[0, 0], theta), (coupling_ref.at[0, 0], coupling),
            (edge_ref.at[0], edge), (transfer_ref.at[0, 0], own_step), (right_ref.at[0, 0], right),
        ))
    ]
    for load in loads:
        load.start()

    barrier = pltpu.get_barrier_semaphore()
    for d in range(1, n_seg):
        pl.semaphore_signal(
            barrier, inc=1, device_id=(lax.rem(seg + d, n_seg), me), device_id_type=MESH
        )
    for d in range(1, n_op):
        pl.semaphore_signal(
            barrier, inc=1, device_id=(seg, lax.rem(me + d, n_op)), device_id_type=MESH
        )

    live_rows = lax.broadcasted_iota(jnp.int32, (size, width), 0) < rows_ref[0]

    def live(c):
        cols = lax.broadcasted_iota(jnp.int32, (size, width), 1) + c * width
        return live_rows & (cols < cols_ref[0])

    loads[0].wait()
    for c in range(CHUNKS):
        cs = pl.ds(c * width, width)
        field[0, c] = jnp.where(live(c), theta[:, cs].astype(f32), 0.0).astype(bf16)

    pl.semaphore_wait(barrier, n_seg + n_op - 2)

    def t_copy(d):
        return pltpu.make_async_remote_copy(
            src_ref=transfer_ref.at[0, 0], dst_ref=arrived.at[seg],
            send_sem=t_send.at[d], recv_sem=t_recv.at[seg],
            device_id=(seg + d, me), device_id_type=MESH,
        )

    quarter = size // 4

    def rows_of(i):
        return pl.ds(i * quarter, quarter)

    def l_copy(i, path, target):
        part = first_left.at[rows_of(i), pl.ds(i * quarter, size - i * quarter)]
        return pltpu.make_async_remote_copy(
            src_ref=part, dst_ref=part, send_sem=l_send.at[path, i], recv_sem=l_recv.at[i],
            device_id=(target, me), device_id_type=MESH,
        )

    def step_copy(i, sem, target, forwarded):
        part = arrived.at[1, rows_of(i)]
        return pltpu.make_async_remote_copy(
            src_ref=part if forwarded else transfer_ref.at[0, 0, rows_of(i)], dst_ref=part,
            send_sem=t_send.at[sem], recv_sem=t_recv.at[i],
            device_id=(target, me), device_id_type=MESH,
        )

    def last_copy():
        return pltpu.make_async_remote_copy(
            src_ref=transfer_ref.at[0, 0], dst_ref=arrived.at[2],
            send_sem=t_send.at[4], recv_sem=t_recv.at[4],
            device_id=(3, me), device_id_type=MESH,
        )

    if square:
        @pl.when(seg == 1)
        def _():
            for i in (1, 2, 3):
                step_copy(i, i, 3, False).start()
            step_copy(0, 4, 0, False).start()
            step_copy(0, 0, 3, False).start()

        @pl.when(seg == 2)
        def _():
            last_copy().start()
    else:
        for d in range(1, n_seg):
            @pl.when(seg + d < n_seg)
            def _():
                t_copy(d).start()

    def up_copy(step, c):
        return pltpu.make_async_remote_copy(
            src_ref=field.at[step, c], dst_ref=prev.at[step, c],
            send_sem=field_send.at[step, 0, c], recv_sem=prev_recv.at[step, c],
            device_id=(seg, me + 1), device_id_type=MESH,
        )

    def down_copy(step, c):
        return pltpu.make_async_remote_copy(
            src_ref=field.at[step, c], dst_ref=foll.at[step, c],
            send_sem=field_send.at[step, 1, c], recv_sem=foll_recv.at[step, c],
            device_id=(seg, me - 1), device_id_type=MESH,
        )

    def send_field(step, c):
        @pl.when(has_next)
        def _():
            up_copy(step, c).start()

        @pl.when(has_prev)
        def _():
            down_copy(step, c).start()

    def take_field(step, c):
        @pl.when(has_prev)
        def _():
            up_copy(step, c).wait_recv()

        @pl.when(has_next)
        def _():
            down_copy(step, c).wait_recv()

    def settle_field(step, c):
        @pl.when(has_next)
        def _():
            up_copy(step, c).wait_send()

        @pl.when(has_prev)
        def _():
            down_copy(step, c).wait_send()

    def coupling_copy():
        return pltpu.make_async_remote_copy(
            src_ref=coupling_ref.at[0, 0], dst_ref=next_coupling,
            send_sem=c_send, recv_sem=c_recv,
            device_id=(seg, me - 1), device_id_type=MESH,
        )

    for c in range(CHUNKS):
        send_field(0, c)

    @pl.when(has_prev)
    def _():
        coupling_copy().start()

    def sum_copy(rnd, d):
        return pltpu.make_async_remote_copy(
            src_ref=sums.at[rnd, me], dst_ref=sums.at[rnd, me],
            send_sem=sum_send.at[rnd, d], recv_sem=sum_recv.at[rnd, me],
            device_id=(seg, lax.rem(me + d, n_op)), device_id_type=MESH,
        )

    def sum_start(rnd, parts):
        row = lax.broadcasted_iota(jnp.int32, (8, 128), 0)
        tile = jnp.zeros((8, 128), f32)
        for i, part in enumerate(parts):
            tile = jnp.where(row == i, part, tile)
        sums[rnd, me] = tile
        for d in range(1, n_op):
            sum_copy(rnd, d).start()

    def sum_finish(rnd, count):
        for d in range(1, n_op):
            source = lax.rem(me + d, n_op)
            pltpu.make_async_remote_copy(
                src_ref=sums.at[rnd, source], dst_ref=sums.at[rnd, source],
                send_sem=sum_send.at[rnd, d], recv_sem=sum_recv.at[rnd, source],
                device_id=(seg, source), device_id_type=MESH,
            ).wait_recv()
        total = sums[rnd, 0]
        for p in range(1, n_op):
            total = total + sums[rnd, p]
        total = jnp.sum(total, axis=1, keepdims=True)
        return [total[i : i + 1] for i in range(count)]

    def sum_settle(rnd):
        for d in range(1, n_op):
            sum_copy(rnd, d).wait_send()

    start_part = jnp.zeros((1, 128), f32)
    for c in range(CHUNKS):
        wide = field[0, c].astype(f32)
        start_part += folded(wide * wide)
    sum_start(0, [start_part])

    for load in loads[1:]:
        load.wait()
    edge_wide = edge[...].astype(f32)
    left_wide[...] = 0.5 * (edge_wide + edge_wide.T)

    def flip(step):
        flipped[...] = step.astype(f32).T.astype(bf16)

    def advance(left, step):
        if left.dtype == bf16:
            image = mm(left, step)
        else:
            high, rest = split(left)
            image = mm(high, step) + mm(rest, step)
        high, rest = split(image)
        return mm(flipped[...], high) + mm(flipped[...], rest)

    def mirror():
        for i in range(4):
            for j in range(i + 1, 4):
                block = first_left[rows_of(i), rows_of(j)].astype(f32)
                first_left[rows_of(j), rows_of(i)] = block.T.astype(bf16)

    if square:
        @pl.when(seg == 0)
        def _():
            flip(own_step[...])
            first_left[...] = advance(left_wide[...], own_step[...]).astype(bf16)
            for i in range(4):
                l_copy(i, 0, 1).start()
                l_copy(i, 1, 2).start()
            step_copy(0, 0, 2, True).wait_recv()
            step_copy(0, 0, 2, True).start()

        for here, turns in ((1, (0, 3)), (2, (1, 2))):
            @pl.when(seg == here)
            def _():
                for i in turns:
                    l_copy(i, 0, 3).wait_recv()
                    l_copy(i, 0, 3).start()

        @pl.when(seg == 3)
        def _():
            for i in (1, 2, 3):
                step_copy(i, i, 2, True).wait_recv()
                step_copy(i, i, 2, True).start()

    right_wide = right[...].astype(f32)
    right_blk[...] = (0.5 * (right_wide + right_wide.T)).astype(bf16)

    @pl.when(jnp.logical_not(has_prev))
    def _():
        prev[...] = jnp.zeros_like(prev)

    @pl.when(jnp.logical_not(has_next))
    def _():
        foll[...] = jnp.zeros_like(foll)
        lifted_coupling[...] = jnp.zeros_like(lifted_coupling)

    (start_total,) = sum_finish(0, 1)
    start_norm = jnp.sqrt(start_total + epsilon)

    @pl.when(has_next)
    def _():
        down = coupling_copy()
        down.wait_recv()
        lifted_coupling[...] = next_coupling[...].astype(f32).T.astype(bf16)

    for c in range(CHUNKS):
        vec[c] = field[0, c].astype(f32) / start_norm
        take_field(0, c)
        before = (prev[0, c].astype(f32) / start_norm).astype(bf16)
        after = (foll[0, c].astype(f32) / start_norm).astype(bf16)
        app[c] = mm(coupling[...], before) + mm(lifted_coupling[...], after)

    if square:
        @pl.when(seg == 1)
        def _():
            for i in (1, 2):
                l_copy(i, 0, 3).wait_recv()
            mirror()
            left_wide[...] = first_left[...].astype(f32)

        @pl.when(seg == 2)
        def _():
            for i in range(4):
                step_copy(i, 0, 3, True).wait_recv()
            flip(arrived[1])
            for i in (0, 3):
                l_copy(i, 0, 3).wait_recv()
            mirror()
            left_wide[...] = advance(first_left[...], arrived[1])

        @pl.when(seg == 3)
        def _():
            step_copy(0, 0, 2, True).wait_recv()
            flip(arrived[1])
            for i in range(4):
                l_copy(i, 0, 3).wait_recv()
            mirror()
            left_wide[...] = advance(first_left[...], arrived[1])
            last_copy().wait_recv()
            flip(arrived[2])
            left_wide[...] = advance(left_wide[...], arrived[2])
    else:
        for j in range(n_seg - 1):
            @pl.when(j < seg)
            def _():
                pltpu.make_async_remote_copy(
                    src_ref=transfer_ref.at[0, 0], dst_ref=arrived.at[j],
                    send_sem=t_send.at[0], recv_sem=t_recv.at[j],
                    device_id=(seg - 1, me), device_id_type=MESH,
                ).wait_recv()
                flip(arrived[j])
                left_wide[...] = advance(left_wide[...], arrived[j])

    left_out[0, 0] = left_wide[...].astype(bf16)

    for c in range(CHUNKS):
        cs = pl.ds(c * width, width)
        middle[:, cs] = mm(left_out[0, 0], vec[c].astype(bf16)).astype(bf16)
    block = size // ROW_BLOCKS
    zero = jnp.zeros((1, 128), f32)

    def passes(body, sums_count):
        def one(i, parts):
            found = body(pl.ds(pl.multiple_of(i * block, block), block))
            return tuple(p + folded8(x) for p, x in zip(parts, found))

        start = tuple(jnp.zeros((8, 128), f32) for _ in range(sums_count))
        parts = lax.fori_loop(0, ROW_BLOCKS, one, start)
        return [jnp.sum(p, axis=0, keepdims=True) for p in parts]

    def live_block(c, rows):
        row = lax.broadcasted_iota(jnp.int32, (block, width), 0) + rows.start
        col = lax.broadcasted_iota(jnp.int32, (block, width), 1) + c * width
        return (row < rows_ref[0]) & (col < cols_ref[0])

    def diagonal(step):
        for c in range(CHUNKS):
            cs = pl.ds(c * width, width)
            high, rest = split(mm(left_out[0, 0], field[step, c]) + mm(left_out[0, 0], low[c]))
            middle[:, cs] = high
            middle_low[:, cs] = rest
        for c in range(CHUNKS):
            cs = pl.ds(c * width, width)
            app[c] = mm(middle[...], right_blk[:, cs]) + mm(middle_low[...], right_blk[:, cs])

    def hop(step, c):
        take_field(step, c)
        app[c] += mm(coupling[...], prev[step, c]) + mm(lifted_coupling[...], foll[step, c])

    energy_part = zero
    for c in range(CHUNKS):
        cs = pl.ds(c * width, width)
        app[c] += mm(middle[...], right_blk[:, cs])

        def first_pass(rows):
            image = jnp.where(live_block(c, rows), app[c, rows], 0.0)
            img[c, rows] = image
            high, rest = split(image)
            field[1, c, rows] = high
            low[c, rows] = rest
            return (vec[c, rows] * image,)

        (part,) = passes(first_pass, 1)
        energy_part += part
        if c == CHUNKS - 1:
            sum_start(1, [energy_part])
        send_field(1, c)
    diagonal(1)
    (energy,) = sum_finish(1, 1)
    first_out[0] = energy[0, 0]
    level[...] = jnp.broadcast_to(energy, level.shape)

    totals = [zero, zero, zero]
    for c in range(CHUNKS):
        hop(1, c)

        def second_pass(rows):
            twice = jnp.where(live_block(c, rows), app[c, rows], 0.0)
            him[c, rows] = twice
            image = img[c, rows]
            corr = image - energy * vec[c, rows]
            applied = twice - energy * image
            high, rest = split(applied)
            field[2, c, rows] = high
            low[c, rows] = rest
            return corr * corr, image * corr, corr * applied

        totals = [t + p for t, p in zip(totals, passes(second_pass, 3))]
        if c == CHUNKS - 1:
            sum_start(2, totals)
        send_field(2, c)

    def rotate(step):
        energy = level[0:1, 0:1]
        corr_norm, cross_term, curv_term = sum_finish(step + 1, 3)
        scale_norm = jnp.sqrt(corr_norm + epsilon)
        offdiag = cross_term / scale_norm
        diag_value = curv_term / (corr_norm + epsilon)
        half_gap = (diag_value - energy) / 2
        lowest = (energy + diag_value) / 2 - jnp.sqrt(half_gap * half_gap + offdiag * offdiag)
        rotation = lowest - energy
        radius = jnp.sqrt(offdiag * offdiag + rotation * rotation + epsilon)
        level[...] = jnp.broadcast_to(lowest, level.shape)
        return energy, lowest, offdiag / radius, rotation / scale_norm / radius

    def sweep(step, carry):
        diagonal(step + 1)
        energy, lowest, keep, turn = rotate(step)
        totals = [zero, zero, zero]
        for c in range(CHUNKS):
            hop(step + 1, c)

            def update(rows):
                vector, image, twice = vec[c, rows], img[c, rows], him[c, rows]
                more = jnp.where(live_block(c, rows), app[c, rows], 0.0)
                corr = image - energy * vector
                applied = twice - energy * image
                vector = keep * vector + turn * corr
                image = keep * image + turn * applied
                twice = keep * twice + turn * more
                vec[c, rows] = vector
                img[c, rows] = image
                him[c, rows] = twice
                corr = image - lowest * vector
                applied = twice - lowest * image
                high, rest = split(applied)
                field[step + 2, c, rows] = high
                low[c, rows] = rest
                return corr * corr, image * corr, corr * applied

            totals = [t + p for t, p in zip(totals, passes(update, 3))]
            if c == CHUNKS - 1:
                sum_start(step + 2, totals)

            @pl.when(step < DAVIDSON - 1)
            def _():
                send_field(step + 2, c)

            settle_field(step + 1, c)
        sum_settle(step + 1)
        return carry

    lax.fori_loop(1, DAVIDSON, sweep, 0)
    energy, lowest, keep, turn = rotate(DAVIDSON)
    for c in range(CHUNKS):
        cs = pl.ds(c * width, width)

        def last_pass(rows):
            vector = vec[c, rows]
            corr = img[c, rows] - energy * vector
            vec_out[0, 0, rows, cs] = keep * vector + turn * corr
            return ()

        passes(last_pass, 0)
    energy_out[0] = lowest[0, 0]
    sum_settle(DAVIDSON + 1)

    if square:
        @pl.when(seg == 0)
        def _():
            for i in range(4):
                l_copy(i, 0, 1).wait_send()
                l_copy(i, 1, 2).wait_send()
            step_copy(0, 0, 2, True).wait_send()

        @pl.when(seg == 1)
        def _():
            for i in range(4):
                step_copy(i, i, 3, False).wait_send()
            step_copy(0, 4, 0, False).wait_send()

        for here, turns in ((1, (0, 3)), (2, (1, 2))):
            @pl.when(seg == here)
            def _():
                for i in turns:
                    l_copy(i, 0, 3).wait_send()

        @pl.when(seg == 2)
        def _():
            last_copy().wait_send()

        @pl.when(seg == 3)
        def _():
            for i in (1, 2, 3):
                step_copy(i, i, 2, True).wait_send()
    else:
        for d in range(1, n_seg):
            @pl.when(seg + d < n_seg)
            def _():
                t_copy(d).wait_send()
    for c in range(CHUNKS):
        settle_field(0, c)
        settle_field(1, c)

    @pl.when(has_prev)
    def _():
        coupling_copy().wait_send()

    sum_settle(0)
    sum_settle(1)


def on_device(n_seg, n_op, *arrays):
    size = arrays[0].shape[-1]
    width = size // CHUNKS
    vmem = pl.BlockSpec(memory_space=pltpu.VMEM)
    smem = pl.BlockSpec(memory_space=pltpu.SMEM)
    dma = pltpu.SemaphoreType.DMA
    fields = (STEPS, CHUNKS, size, width)
    return pl.pallas_call(
        functools.partial(kernel, n_seg, n_op),
        out_shape=(
            jax.ShapeDtypeStruct((1, 1, size, size), f32),
            jax.ShapeDtypeStruct((1, 1, size, size), bf16),
            jax.ShapeDtypeStruct((1,), f32),
            jax.ShapeDtypeStruct((1,), f32),
        ),
        in_specs=[pl.BlockSpec(memory_space=pltpu.HBM)] * 5 + [smem] * 2,
        out_specs=(vmem, vmem, smem, smem),
        scratch_shapes=[
            pltpu.VMEM((size, size), bf16),
            pltpu.VMEM((size, size), bf16),
            pltpu.VMEM((size, size), bf16),
            pltpu.VMEM((size, size), bf16),
            pltpu.VMEM((size, size), bf16),
            pltpu.VMEM((size, size), bf16),
            pltpu.VMEM((size, size), bf16),
            pltpu.VMEM(fields, bf16),
            pltpu.VMEM(fields, bf16),
            pltpu.VMEM(fields, bf16),
            pltpu.VMEM((size, size), bf16),
            pltpu.VMEM((size, size), bf16),
            pltpu.VMEM((n_seg - 1, size, size), bf16),
            pltpu.VMEM((size, size), f32),
            pltpu.VMEM((size, size), bf16),
            pltpu.VMEM((size, size), bf16),
            pltpu.VMEM((size, size), bf16),
            pltpu.VMEM((CHUNKS, size, width), bf16),
            pltpu.VMEM((CHUNKS, size, width), f32),
            pltpu.VMEM((CHUNKS, size, width), f32),
            pltpu.VMEM((CHUNKS, size, width), f32),
            pltpu.VMEM((CHUNKS, size, width), f32),
            pltpu.VMEM((ROUNDS, n_op, 8, 128), f32),
            pltpu.VMEM((8, 128), f32),
            dma((5,)),
            dma((2, 4)),
            dma((4,)),
            dma((STEPS, 2, CHUNKS)),
            dma((STEPS, CHUNKS)),
            dma((STEPS, CHUNKS)),
            dma((n_seg + 1,)),
            dma((n_seg + 1,)),
            dma,
            dma,
            dma((ROUNDS, n_op)),
            dma((ROUNDS, n_op)),
        ],
        compiler_params=pltpu.CompilerParams(
            collective_id=0, has_side_effects=True, vmem_limit_bytes=VMEM_LIMIT
        ),
        cost_estimate=pl.CostEstimate(
            flops=2 * 30 * size**3, bytes_accessed=8 * size * size * 2, transcendentals=0
        ),
        name="segment_solve",
    )(*arrays)


def solution(mesh):
    placed = (
        P("seg", "op", None, None),
        P("op", None, None),
        P("seg", "op", None, None),
        P("seg", "op", None, None),
        P("seg", "op", None, None),
        P("op"),
        P("op"),
    )
    return jax.shard_map(
        functools.partial(on_device, mesh.shape["seg"], mesh.shape["op"]),
        mesh=mesh,
        in_specs=placed,
        out_specs=(P("seg", "op", None, None), P("seg", "op", None, None), P("seg"), P("seg")),
        check_vma=False,
    )
```

```python
import functools

import jax
import jax.numpy as jnp
from jax import lax
from jax.experimental import pallas as pl
from jax.experimental.pallas import tpu as pltpu
from jax.sharding import PartitionSpec as P

DAVIDSON = 4
STEPS = DAVIDSON + 2
ROUNDS = DAVIDSON + 2
CHUNKS = 2
ROW_BLOCKS = 16
VMEM_LIMIT = 63 * 1024 * 1024

epsilon = 1e-06

MESH = pl.DeviceIdType.MESH
f32 = jnp.float32
bf16 = jnp.bfloat16


def mm(a, b):
    return jnp.dot(a, b, preferred_element_type=f32)


def split(x):
    high = x.astype(bf16)
    return high, (x - high.astype(f32)).astype(bf16)


def folded8(x):
    rows, width = x.shape
    x = jnp.sum(x.reshape(rows // 8, 8, width), axis=0)
    acc = x[:, :128]
    for start in range(128, width, 128):
        acc = acc + x[:, start : start + 128]
    return acc


def folded(x):
    return jnp.sum(folded8(x), axis=0, keepdims=True)


def kernel(
    n_seg, n_op,
    theta_ref, edge_ref, transfer_ref, right_ref, coupling_ref, rows_ref, cols_ref,
    vec_out, left_out, energy_out, first_out,
    theta, edge, right, coupling, own_step, first_left, flipped,
    field, prev, foll, next_coupling, lifted_coupling, arrived, left_wide, right_blk,
    middle, vec, img, him, app, sums, level,
    load_sem, l_send, l_recv, field_send, prev_recv, foll_recv, t_send, t_recv, c_send, c_recv, sum_send, sum_recv,
):
    seg = lax.axis_index("seg")
    me = lax.axis_index("op")
    size = theta_ref.shape[-1]
    width = size // CHUNKS
    square = n_seg == 4
    has_prev = me > 0
    has_next = me < n_op - 1

    loads = [
        pltpu.make_async_copy(ref, held, load_sem.at[i])
        for i, (ref, held) in enumerate((
            (theta_ref.at[0, 0], theta), (coupling_ref.at[0, 0], coupling),
            (edge_ref.at[0], edge), (transfer_ref.at[0, 0], own_step), (right_ref.at[0, 0], right),
        ))
    ]
    for load in loads:
        load.start()

    barrier = pltpu.get_barrier_semaphore()
    for d in range(1, n_seg):
        pl.semaphore_signal(
            barrier, inc=1, device_id=(lax.rem(seg + d, n_seg), me), device_id_type=MESH
        )
    for d in range(1, n_op):
        pl.semaphore_signal(
            barrier, inc=1, device_id=(seg, lax.rem(me + d, n_op)), device_id_type=MESH
        )

    live_rows = lax.broadcasted_iota(jnp.int32, (size, width), 0) < rows_ref[0]

    def live(c):
        cols = lax.broadcasted_iota(jnp.int32, (size, width), 1) + c * width
        return live_rows & (cols < cols_ref[0])

    loads[0].wait()
    for c in range(CHUNKS):
        cs = pl.ds(c * width, width)
        field[0, c] = jnp.where(live(c), theta[:, cs].astype(f32), 0.0).astype(bf16)

    pl.semaphore_wait(barrier, n_seg + n_op - 2)

    def t_copy(d):
        return pltpu.make_async_remote_copy(
            src_ref=transfer_ref.at[0, 0], dst_ref=arrived.at[seg],
            send_sem=t_send.at[d], recv_sem=t_recv.at[seg],
            device_id=(seg + d, me), device_id_type=MESH,
        )

    quarter = size // 4

    def rows_of(i):
        return pl.ds(i * quarter, quarter)

    def l_copy(i, path, target):
        part = first_left.at[rows_of(i), pl.ds(i * quarter, size - i * quarter)]
        return pltpu.make_async_remote_copy(
            src_ref=part, dst_ref=part, send_sem=l_send.at[path, i], recv_sem=l_recv.at[i],
            device_id=(target, me), device_id_type=MESH,
        )

    def step_copy(i, sem, target, forwarded):
        part = arrived.at[1, rows_of(i)]
        return pltpu.make_async_remote_copy(
            src_ref=part if forwarded else transfer_ref.at[0, 0, rows_of(i)], dst_ref=part,
            send_sem=t_send.at[sem], recv_sem=t_recv.at[i],
            device_id=(target, me), device_id_type=MESH,
        )

    def last_copy():
        return pltpu.make_async_remote_copy(
            src_ref=transfer_ref.at[0, 0], dst_ref=arrived.at[2],
            send_sem=t_send.at[4], recv_sem=t_recv.at[4],
            device_id=(3, me), device_id_type=MESH,
        )

    if square:
        @pl.when(seg == 1)
        def _():
            for i in (1, 2, 3):
                step_copy(i, i, 3, False).start()
            step_copy(0, 4, 0, False).start()
            step_copy(0, 0, 3, False).start()

        @pl.when(seg == 2)
        def _():
            last_copy().start()
    else:
        for d in range(1, n_seg):
            @pl.when(seg + d < n_seg)
            def _():
                t_copy(d).start()

    def up_copy(step, c):
        return pltpu.make_async_remote_copy(
            src_ref=field.at[step, c], dst_ref=prev.at[step, c],
            send_sem=field_send.at[step, 0, c], recv_sem=prev_recv.at[step, c],
            device_id=(seg, me + 1), device_id_type=MESH,
        )

    def down_copy(step, c):
        return pltpu.make_async_remote_copy(
            src_ref=field.at[step, c], dst_ref=foll.at[step, c],
            send_sem=field_send.at[step, 1, c], recv_sem=foll_recv.at[step, c],
            device_id=(seg, me - 1), device_id_type=MESH,
        )

    def send_field(step, c):
        @pl.when(has_next)
        def _():
            up_copy(step, c).start()

        @pl.when(has_prev)
        def _():
            down_copy(step, c).start()

    def take_field(step, c):
        @pl.when(has_prev)
        def _():
            up_copy(step, c).wait_recv()

        @pl.when(has_next)
        def _():
            down_copy(step, c).wait_recv()

    def settle_field(step, c):
        @pl.when(has_next)
        def _():
            up_copy(step, c).wait_send()

        @pl.when(has_prev)
        def _():
            down_copy(step, c).wait_send()

    def coupling_copy():
        return pltpu.make_async_remote_copy(
            src_ref=coupling_ref.at[0, 0], dst_ref=next_coupling,
            send_sem=c_send, recv_sem=c_recv,
            device_id=(seg, me - 1), device_id_type=MESH,
        )

    for c in range(CHUNKS):
        send_field(0, c)

    @pl.when(has_prev)
    def _():
        coupling_copy().start()

    def sum_copy(rnd, d):
        return pltpu.make_async_remote_copy(
            src_ref=sums.at[rnd, me], dst_ref=sums.at[rnd, me],
            send_sem=sum_send.at[rnd, d], recv_sem=sum_recv.at[rnd, me],
            device_id=(seg, lax.rem(me + d, n_op)), device_id_type=MESH,
        )

    def sum_start(rnd, parts):
        row = lax.broadcasted_iota(jnp.int32, (8, 128), 0)
        tile = jnp.zeros((8, 128), f32)
        for i, part in enumerate(parts):
            tile = jnp.where(row == i, part, tile)
        tile = jnp.sum(tile, axis=1, keepdims=True)
        lane = lax.broadcasted_iota(jnp.int32, (8, 128), 1)
        sums[rnd, me] = jnp.sum(jnp.where(lane == row, tile, 0.0), axis=0, keepdims=True)
        for d in range(1, n_op):
            sum_copy(rnd, d).start()

    def sum_finish(rnd, count):
        for d in range(1, n_op):
            source = lax.rem(me + d, n_op)
            pltpu.make_async_remote_copy(
                src_ref=sums.at[rnd, source], dst_ref=sums.at[rnd, source],
                send_sem=sum_send.at[rnd, d], recv_sem=sum_recv.at[rnd, source],
                device_id=(seg, source), device_id_type=MESH,
            ).wait_recv()
        total = sums[rnd, 0]
        for p in range(1, n_op):
            total = total + sums[rnd, p]
        return [total[:, i : i + 1] for i in range(count)]

    def sum_settle(rnd):
        for d in range(1, n_op):
            sum_copy(rnd, d).wait_send()

    start_part = jnp.zeros((1, 128), f32)
    for c in range(CHUNKS):
        wide = field[0, c].astype(f32)
        start_part += folded(wide * wide)
    sum_start(0, [start_part])

    for load in loads[1:]:
        load.wait()
    edge_wide = edge[...].astype(f32)
    left_wide[...] = 0.5 * (edge_wide + edge_wide.T)

    def flip(step):
        flipped[...] = step.astype(f32).T.astype(bf16)

    def advance(left, step):
        if left.dtype == bf16:
            image = mm(left, step)
        else:
            high, rest = split(left)
            image = mm(high, step) + mm(rest, step)
        high, rest = split(image)
        return mm(flipped[...], high) + mm(flipped[...], rest)

    def mirror():
        for i in range(4):
            for j in range(i + 1, 4):
                block = first_left[rows_of(i), rows_of(j)].astype(f32)
                first_left[rows_of(j), rows_of(i)] = block.T.astype(bf16)

    if square:
        @pl.when(seg == 0)
        def _():
            flip(own_step[...])
            first_left[...] = advance(left_wide[...], own_step[...]).astype(bf16)
            for i in range(4):
                l_copy(i, 0, 1).start()
                l_copy(i, 1, 2).start()
            step_copy(0, 0, 2, True).wait_recv()
            step_copy(0, 0, 2, True).start()

        for here, turns in ((1, (0, 3)), (2, (1, 2))):
            @pl.when(seg == here)
            def _():
                for i in turns:
                    l_copy(i, 0, 3).wait_recv()
                    l_copy(i, 0, 3).start()

        @pl.when(seg == 3)
        def _():
            for i in (1, 2, 3):
                step_copy(i, i, 2, True).wait_recv()
                step_copy(i, i, 2, True).start()

    right_wide = right[...].astype(f32)
    right_blk[...] = (0.5 * (right_wide + right_wide.T)).astype(bf16)

    @pl.when(jnp.logical_not(has_prev))
    def _():
        prev[...] = jnp.zeros_like(prev)

    @pl.when(jnp.logical_not(has_next))
    def _():
        foll[...] = jnp.zeros_like(foll)
        lifted_coupling[...] = jnp.zeros_like(lifted_coupling)

    (start_total,) = sum_finish(0, 1)
    start_norm = jnp.sqrt(start_total + epsilon)

    @pl.when(has_next)
    def _():
        down = coupling_copy()
        down.wait_recv()
        lifted_coupling[...] = next_coupling[...].astype(f32).T.astype(bf16)

    for c in range(CHUNKS):
        vec[c] = field[0, c].astype(f32) / start_norm
        take_field(0, c)
        before = (prev[0, c].astype(f32) / start_norm).astype(bf16)
        after = (foll[0, c].astype(f32) / start_norm).astype(bf16)
        app[c] = mm(coupling[...], before) + mm(lifted_coupling[...], after)

    if square:
        @pl.when(seg == 1)
        def _():
            for i in (1, 2):
                l_copy(i, 0, 3).wait_recv()
            mirror()
            left_wide[...] = first_left[...].astype(f32)

        @pl.when(seg == 2)
        def _():
            for i in range(4):
                step_copy(i, 0, 3, True).wait_recv()
            flip(arrived[1])
            for i in (0, 3):
                l_copy(i, 0, 3).wait_recv()
            mirror()
            left_wide[...] = advance(first_left[...], arrived[1])

        @pl.when(seg == 3)
        def _():
            step_copy(0, 0, 2, True).wait_recv()
            flip(arrived[1])
            for i in range(4):
                l_copy(i, 0, 3).wait_recv()
            mirror()
            left_wide[...] = advance(first_left[...], arrived[1])
            last_copy().wait_recv()
            flip(arrived[2])
            left_wide[...] = advance(left_wide[...], arrived[2])
    else:
        for j in range(n_seg - 1):
            @pl.when(j < seg)
            def _():
                pltpu.make_async_remote_copy(
                    src_ref=transfer_ref.at[0, 0], dst_ref=arrived.at[j],
                    send_sem=t_send.at[0], recv_sem=t_recv.at[j],
                    device_id=(seg - 1, me), device_id_type=MESH,
                ).wait_recv()
                flip(arrived[j])
                left_wide[...] = advance(left_wide[...], arrived[j])

    left_out[0, 0] = left_wide[...].astype(bf16)

    for c in range(CHUNKS):
        cs = pl.ds(c * width, width)
        middle[:, cs] = mm(left_out[0, 0], vec[c].astype(bf16)).astype(bf16)
    block = size // ROW_BLOCKS
    zero = jnp.zeros((1, 128), f32)

    def passes(body, sums_count):
        def one(i, parts):
            found = body(pl.ds(pl.multiple_of(i * block, block), block))
            return tuple(p + folded8(x) for p, x in zip(parts, found))

        start = tuple(jnp.zeros((8, 128), f32) for _ in range(sums_count))
        parts = lax.fori_loop(0, ROW_BLOCKS, one, start)
        return [jnp.sum(p, axis=0, keepdims=True) for p in parts]

    def live_block(c, rows):
        row = lax.broadcasted_iota(jnp.int32, (block, width), 0) + rows.start
        col = lax.broadcasted_iota(jnp.int32, (block, width), 1) + c * width
        return (row < rows_ref[0]) & (col < cols_ref[0])

    def diagonal(step):
        for c in range(CHUNKS):
            cs = pl.ds(c * width, width)
            middle[:, cs] = mm(left_out[0, 0], field[step, c]).astype(bf16)
        for c in range(CHUNKS):
            cs = pl.ds(c * width, width)
            app[c] = mm(middle[...], right_blk[:, cs])

    def hop(step, c):
        take_field(step, c)
        app[c] += mm(coupling[...], prev[step, c]) + mm(lifted_coupling[...], foll[step, c])

    energy_part = zero
    for c in range(CHUNKS):
        cs = pl.ds(c * width, width)
        app[c] += mm(middle[...], right_blk[:, cs])

        def first_pass(rows):
            image = jnp.where(live_block(c, rows), app[c, rows], 0.0)
            img[c, rows] = image
            field[1, c, rows] = image.astype(bf16)
            return (vec[c, rows] * image,)

        (part,) = passes(first_pass, 1)
        energy_part += part
        if c == CHUNKS - 1:
            sum_start(1, [energy_part])
        send_field(1, c)
    diagonal(1)
    (energy,) = sum_finish(1, 1)
    first_out[0] = energy[0, 0]
    level[...] = jnp.broadcast_to(energy, level.shape)

    totals = [zero, zero, zero]
    for c in range(CHUNKS):
        hop(1, c)

        def second_pass(rows):
            twice = jnp.where(live_block(c, rows), app[c, rows], 0.0)
            him[c, rows] = twice
            image = img[c, rows]
            corr = image - energy * vec[c, rows]
            applied = twice - energy * image
            field[2, c, rows] = applied.astype(bf16)
            return corr * corr, image * corr, corr * applied

        totals = [t + p for t, p in zip(totals, passes(second_pass, 3))]
        if c == CHUNKS - 1:
            sum_start(2, totals)
        send_field(2, c)

    def rotate(step):
        energy = level[0:1, 0:1]
        corr_norm, cross_term, curv_term = sum_finish(step + 1, 3)
        scale_norm = jnp.sqrt(corr_norm + epsilon)
        offdiag = cross_term / scale_norm
        diag_value = curv_term / (corr_norm + epsilon)
        half_gap = (diag_value - energy) / 2
        lowest = (energy + diag_value) / 2 - jnp.sqrt(half_gap * half_gap + offdiag * offdiag)
        rotation = lowest - energy
        radius = jnp.sqrt(offdiag * offdiag + rotation * rotation + epsilon)
        level[...] = jnp.broadcast_to(lowest, level.shape)
        return energy, lowest, offdiag / radius, rotation / scale_norm / radius

    def sweep(step, carry):
        diagonal(step + 1)
        energy, lowest, keep, turn = rotate(step)
        stay = keep - turn * energy
        totals = [zero, zero, zero]
        for c in range(CHUNKS):
            hop(step + 1, c)

            def update(rows):
                vector, image, twice = vec[c, rows], img[c, rows], him[c, rows]
                more = jnp.where(live_block(c, rows), app[c, rows], 0.0)
                vector = stay * vector + turn * image
                image = stay * image + turn * twice
                twice = keep * twice + turn * more
                vec[c, rows] = vector
                img[c, rows] = image
                him[c, rows] = twice
                corr = image - lowest * vector
                applied = twice - lowest * image
                field[step + 2, c, rows] = applied.astype(bf16)
                return corr * corr, image * corr, corr * applied

            totals = [t + p for t, p in zip(totals, passes(update, 3))]
            if c == CHUNKS - 1:
                sum_start(step + 2, totals)

            @pl.when(step < DAVIDSON - 1)
            def _():
                send_field(step + 2, c)

            settle_field(step + 1, c)
        sum_settle(step + 1)
        return carry

    lax.fori_loop(1, DAVIDSON, sweep, 0)
    energy, lowest, keep, turn = rotate(DAVIDSON)
    for c in range(CHUNKS):
        cs = pl.ds(c * width, width)

        def last_pass(rows):
            vector = vec[c, rows]
            corr = img[c, rows] - energy * vector
            vec_out[0, 0, rows, cs] = keep * vector + turn * corr
            return ()

        passes(last_pass, 0)
    energy_out[0] = lowest[0, 0]
    sum_settle(DAVIDSON + 1)

    if square:
        @pl.when(seg == 0)
        def _():
            for i in range(4):
                l_copy(i, 0, 1).wait_send()
                l_copy(i, 1, 2).wait_send()
            step_copy(0, 0, 2, True).wait_send()

        @pl.when(seg == 1)
        def _():
            for i in range(4):
                step_copy(i, i, 3, False).wait_send()
            step_copy(0, 4, 0, False).wait_send()

        for here, turns in ((1, (0, 3)), (2, (1, 2))):
            @pl.when(seg == here)
            def _():
                for i in turns:
                    l_copy(i, 0, 3).wait_send()

        @pl.when(seg == 2)
        def _():
            last_copy().wait_send()

        @pl.when(seg == 3)
        def _():
            for i in (1, 2, 3):
                step_copy(i, i, 2, True).wait_send()
    else:
        for d in range(1, n_seg):
            @pl.when(seg + d < n_seg)
            def _():
                t_copy(d).wait_send()
    for c in range(CHUNKS):
        settle_field(0, c)
        settle_field(1, c)

    @pl.when(has_prev)
    def _():
        coupling_copy().wait_send()

    sum_settle(0)
    sum_settle(1)


def on_device(n_seg, n_op, *arrays):
    size = arrays[0].shape[-1]
    width = size // CHUNKS
    vmem = pl.BlockSpec(memory_space=pltpu.VMEM)
    smem = pl.BlockSpec(memory_space=pltpu.SMEM)
    dma = pltpu.SemaphoreType.DMA
    fields = (STEPS, CHUNKS, size, width)
    return pl.pallas_call(
        functools.partial(kernel, n_seg, n_op),
        out_shape=(
            jax.ShapeDtypeStruct((1, 1, size, size), f32),
            jax.ShapeDtypeStruct((1, 1, size, size), bf16),
            jax.ShapeDtypeStruct((1,), f32),
            jax.ShapeDtypeStruct((1,), f32),
        ),
        in_specs=[pl.BlockSpec(memory_space=pltpu.HBM)] * 5 + [smem] * 2,
        out_specs=(vmem, vmem, smem, smem),
        scratch_shapes=[
            pltpu.VMEM((size, size), bf16),
            pltpu.VMEM((size, size), bf16),
            pltpu.VMEM((size, size), bf16),
            pltpu.VMEM((size, size), bf16),
            pltpu.VMEM((size, size), bf16),
            pltpu.VMEM((size, size), bf16),
            pltpu.VMEM((size, size), bf16),
            pltpu.VMEM(fields, bf16),
            pltpu.VMEM(fields, bf16),
            pltpu.VMEM(fields, bf16),
            pltpu.VMEM((size, size), bf16),
            pltpu.VMEM((size, size), bf16),
            pltpu.VMEM((n_seg - 1, size, size), bf16),
            pltpu.VMEM((size, size), f32),
            pltpu.VMEM((size, size), bf16),
            pltpu.VMEM((size, size), bf16),
            pltpu.VMEM((CHUNKS, size, width), f32),
            pltpu.VMEM((CHUNKS, size, width), f32),
            pltpu.VMEM((CHUNKS, size, width), f32),
            pltpu.VMEM((CHUNKS, size, width), f32),
            pltpu.VMEM((ROUNDS, n_op, 1, 128), f32),
            pltpu.VMEM((8, 128), f32),
            dma((5,)),
            dma((2, 4)),
            dma((4,)),
            dma((STEPS, 2, CHUNKS)),
            dma((STEPS, CHUNKS)),
            dma((STEPS, CHUNKS)),
            dma((n_seg + 1,)),
            dma((n_seg + 1,)),
            dma,
            dma,
            dma((ROUNDS, n_op)),
            dma((ROUNDS, n_op)),
        ],
        compiler_params=pltpu.CompilerParams(
            collective_id=0, has_side_effects=True, vmem_limit_bytes=VMEM_LIMIT
        ),
        cost_estimate=pl.CostEstimate(
            flops=2 * 30 * size**3, bytes_accessed=8 * size * size * 2, transcendentals=0
        ),
        name="segment_solve",
    )(*arrays)


def solution(mesh):
    placed = (
        P("seg", "op", None, None),
        P("op", None, None),
        P("seg", "op", None, None),
        P("seg", "op", None, None),
        P("seg", "op", None, None),
        P("op"),
        P("op"),
    )
    return jax.shard_map(
        functools.partial(on_device, mesh.shape["seg"], mesh.shape["op"]),
        mesh=mesh,
        in_specs=placed,
        out_specs=(P("seg", "op", None, None), P("seg", "op", None, None), P("seg"), P("seg")),
        check_vma=False,
    )
```

```python
import functools

import jax
import jax.numpy as jnp
from jax import lax
from jax.experimental import pallas as pl
from jax.experimental.pallas import tpu as pltpu
from jax.sharding import PartitionSpec as P

DAVIDSON = 4
STEPS = DAVIDSON + 2
ROUNDS = DAVIDSON + 2
CHUNKS = 2
ROW_BLOCKS = 16
VMEM_LIMIT = 63 * 1024 * 1024

epsilon = 1e-06

MESH = pl.DeviceIdType.MESH
f32 = jnp.float32
bf16 = jnp.bfloat16


def mm(a, b):
    return jnp.dot(a, b, preferred_element_type=f32)


def split(x):
    high = x.astype(bf16)
    return high, (x - high.astype(f32)).astype(bf16)


def folded8(x):
    rows, width = x.shape
    x = jnp.sum(x.reshape(rows // 8, 8, width), axis=0)
    acc = x[:, :128]
    for start in range(128, width, 128):
        acc = acc + x[:, start : start + 128]
    return acc


def folded(x):
    return jnp.sum(folded8(x), axis=0, keepdims=True)


def kernel(
    n_seg, n_op,
    theta_ref, edge_ref, transfer_ref, right_ref, coupling_ref, rows_ref, cols_ref,
    vec_out, left_out, energy_out, first_out,
    theta, edge, right, coupling, own_step, first_left, flipped,
    field, prev, foll, next_coupling, lifted_coupling, arrived, left_wide, right_blk,
    middle, vec, img, him, app, sums, level,
    load_sem, l_send, l_recv, field_send, prev_recv, foll_recv, t_send, t_recv, c_send, c_recv, sum_send, sum_recv,
):
    seg = lax.axis_index("seg")
    me = lax.axis_index("op")
    size = theta_ref.shape[-1]
    width = size // CHUNKS
    square = n_seg == 4
    has_prev = me > 0
    has_next = me < n_op - 1

    loads = [
        pltpu.make_async_copy(ref, held, load_sem.at[i])
        for i, (ref, held) in enumerate((
            (theta_ref.at[0, 0], theta), (coupling_ref.at[0, 0], coupling),
            (edge_ref.at[0], edge), (transfer_ref.at[0, 0], own_step), (right_ref.at[0, 0], right),
        ))
    ]
    for load in loads:
        load.start()

    barrier = pltpu.get_barrier_semaphore()
    for d in range(1, n_seg):
        pl.semaphore_signal(
            barrier, inc=1, device_id=(lax.rem(seg + d, n_seg), me), device_id_type=MESH
        )
    for d in range(1, n_op):
        pl.semaphore_signal(
            barrier, inc=1, device_id=(seg, lax.rem(me + d, n_op)), device_id_type=MESH
        )

    live_rows = lax.broadcasted_iota(jnp.int32, (size, width), 0) < rows_ref[0]

    def live(c):
        cols = lax.broadcasted_iota(jnp.int32, (size, width), 1) + c * width
        return live_rows & (cols < cols_ref[0])

    loads[0].wait()
    for c in range(CHUNKS):
        cs = pl.ds(c * width, width)
        field[0, c] = jnp.where(live(c), theta[:, cs].astype(f32), 0.0).astype(bf16)

    pl.semaphore_wait(barrier, n_seg + n_op - 2)

    def t_copy(d):
        return pltpu.make_async_remote_copy(
            src_ref=transfer_ref.at[0, 0], dst_ref=arrived.at[seg],
            send_sem=t_send.at[d], recv_sem=t_recv.at[seg],
            device_id=(seg + d, me), device_id_type=MESH,
        )

    quarter = size // 4

    def rows_of(i):
        return pl.ds(i * quarter, quarter)

    def l_copy(i, path, target):
        part = first_left.at[rows_of(i), pl.ds(i * quarter, size - i * quarter)]
        return pltpu.make_async_remote_copy(
            src_ref=part, dst_ref=part, send_sem=l_send.at[path, i], recv_sem=l_recv.at[i],
            device_id=(target, me), device_id_type=MESH,
        )

    def step_copy(i, sem, target, forwarded):
        part = arrived.at[1, rows_of(i)]
        return pltpu.make_async_remote_copy(
            src_ref=part if forwarded else transfer_ref.at[0, 0, rows_of(i)], dst_ref=part,
            send_sem=t_send.at[sem], recv_sem=t_recv.at[i],
            device_id=(target, me), device_id_type=MESH,
        )

    def last_copy():
        return pltpu.make_async_remote_copy(
            src_ref=transfer_ref.at[0, 0], dst_ref=arrived.at[2],
            send_sem=t_send.at[4], recv_sem=t_recv.at[4],
            device_id=(3, me), device_id_type=MESH,
        )

    if square:
        @pl.when(seg == 1)
        def _():
            for i in (1, 2, 3):
                step_copy(i, i, 3, False).start()
            step_copy(0, 4, 0, False).start()
            step_copy(0, 0, 3, False).start()

        @pl.when(seg == 2)
        def _():
            last_copy().start()
    else:
        for d in range(1, n_seg):
            @pl.when(seg + d < n_seg)
            def _():
                t_copy(d).start()

    def up_copy(step, c):
        return pltpu.make_async_remote_copy(
            src_ref=field.at[step, c], dst_ref=prev.at[step, c],
            send_sem=field_send.at[step, 0, c], recv_sem=prev_recv.at[step, c],
            device_id=(seg, me + 1), device_id_type=MESH,
        )

    def down_copy(step, c):
        return pltpu.make_async_remote_copy(
            src_ref=field.at[step, c], dst_ref=foll.at[step, c],
            send_sem=field_send.at[step, 1, c], recv_sem=foll_recv.at[step, c],
            device_id=(seg, me - 1), device_id_type=MESH,
        )

    def send_field(step, c):
        @pl.when(has_next)
        def _():
            up_copy(step, c).start()

        @pl.when(has_prev)
        def _():
            down_copy(step, c).start()

    def take_field(step, c):
        @pl.when(has_prev)
        def _():
            up_copy(step, c).wait_recv()

        @pl.when(has_next)
        def _():
            down_copy(step, c).wait_recv()

    def settle_field(step, c):
        @pl.when(has_next)
        def _():
            up_copy(step, c).wait_send()

        @pl.when(has_prev)
        def _():
            down_copy(step, c).wait_send()

    def coupling_copy():
        return pltpu.make_async_remote_copy(
            src_ref=coupling_ref.at[0, 0], dst_ref=next_coupling,
            send_sem=c_send, recv_sem=c_recv,
            device_id=(seg, me - 1), device_id_type=MESH,
        )

    for c in range(CHUNKS):
        send_field(0, c)

    @pl.when(has_prev)
    def _():
        coupling_copy().start()

    def sum_copy(rnd, d):
        return pltpu.make_async_remote_copy(
            src_ref=sums.at[rnd, me], dst_ref=sums.at[rnd, me],
            send_sem=sum_send.at[rnd, d], recv_sem=sum_recv.at[rnd, me],
            device_id=(seg, lax.rem(me + d, n_op)), device_id_type=MESH,
        )

    def sum_start(rnd, parts):
        row = lax.broadcasted_iota(jnp.int32, (8, 128), 0)
        tile = jnp.zeros((8, 128), f32)
        for i, part in enumerate(parts):
            tile = jnp.where(row == i, part, tile)
        sums[rnd, me] = tile
        for d in range(1, n_op):
            sum_copy(rnd, d).start()

    def sum_finish(rnd, count):
        for d in range(1, n_op):
            source = lax.rem(me + d, n_op)
            pltpu.make_async_remote_copy(
                src_ref=sums.at[rnd, source], dst_ref=sums.at[rnd, source],
                send_sem=sum_send.at[rnd, d], recv_sem=sum_recv.at[rnd, source],
                device_id=(seg, source), device_id_type=MESH,
            ).wait_recv()
        total = sums[rnd, 0]
        for p in range(1, n_op):
            total = total + sums[rnd, p]
        total = jnp.sum(total, axis=1, keepdims=True)
        return [total[i : i + 1] for i in range(count)]

    def sum_settle(rnd):
        for d in range(1, n_op):
            sum_copy(rnd, d).wait_send()

    start_part = jnp.zeros((1, 128), f32)
    for c in range(CHUNKS):
        wide = field[0, c].astype(f32)
        start_part += folded(wide * wide)
    sum_start(0, [start_part])

    for load in loads[1:]:
        load.wait()
    edge_wide = edge[...].astype(f32)
    left_wide[...] = 0.5 * (edge_wide + edge_wide.T)

    def flip(step):
        flipped[...] = step.astype(f32).T.astype(bf16)

    def advance(left, step):
        if left.dtype == bf16:
            image = mm(left, step)
        else:
            high, rest = split(left)
            image = mm(high, step) + mm(rest, step)
        high, rest = split(image)
        return mm(flipped[...], high) + mm(flipped[...], rest)

    def mirror():
        for i in range(4):
            for j in range(i + 1, 4):
                block = first_left[rows_of(i), rows_of(j)].astype(f32)
                first_left[rows_of(j), rows_of(i)] = block.T.astype(bf16)

    if square:
        @pl.when(seg == 0)
        def _():
            flip(own_step[...])
            first_left[...] = advance(left_wide[...], own_step[...]).astype(bf16)
            for i in range(4):
                l_copy(i, 0, 1).start()
                l_copy(i, 1, 2).start()
            step_copy(0, 0, 2, True).wait_recv()
            step_copy(0, 0, 2, True).start()

        for here, turns in ((1, (0, 3)), (2, (1, 2))):
            @pl.when(seg == here)
            def _():
                for i in turns:
                    l_copy(i, 0, 3).wait_recv()
                    l_copy(i, 0, 3).start()

        @pl.when(seg == 3)
        def _():
            for i in (1, 2, 3):
                step_copy(i, i, 2, True).wait_recv()
                step_copy(i, i, 2, True).start()

    right_wide = right[...].astype(f32)
    right_blk[...] = (0.5 * (right_wide + right_wide.T)).astype(bf16)

    @pl.when(jnp.logical_not(has_prev))
    def _():
        prev[...] = jnp.zeros_like(prev)

    @pl.when(jnp.logical_not(has_next))
    def _():
        foll[...] = jnp.zeros_like(foll)
        lifted_coupling[...] = jnp.zeros_like(lifted_coupling)

    (start_total,) = sum_finish(0, 1)
    start_norm = jnp.sqrt(start_total + epsilon)

    @pl.when(has_next)
    def _():
        down = coupling_copy()
        down.wait_recv()
        lifted_coupling[...] = next_coupling[...].astype(f32).T.astype(bf16)

    for c in range(CHUNKS):
        vec[c] = field[0, c].astype(f32) / start_norm
        take_field(0, c)
        before = (prev[0, c].astype(f32) / start_norm).astype(bf16)
        after = (foll[0, c].astype(f32) / start_norm).astype(bf16)
        app[c] = mm(coupling[...], before) + mm(lifted_coupling[...], after)

    if square:
        @pl.when(seg == 1)
        def _():
            for i in (1, 2):
                l_copy(i, 0, 3).wait_recv()
            mirror()
            left_wide[...] = first_left[...].astype(f32)

        @pl.when(seg == 2)
        def _():
            for i in range(4):
                step_copy(i, 0, 3, True).wait_recv()
            flip(arrived[1])
            for i in (0, 3):
                l_copy(i, 0, 3).wait_recv()
            mirror()
            left_wide[...] = advance(first_left[...], arrived[1])

        @pl.when(seg == 3)
        def _():
            step_copy(0, 0, 2, True).wait_recv()
            flip(arrived[1])
            for i in range(4):
                l_copy(i, 0, 3).wait_recv()
            mirror()
            left_wide[...] = advance(first_left[...], arrived[1])
            last_copy().wait_recv()
            flip(arrived[2])
            left_wide[...] = advance(left_wide[...], arrived[2])
    else:
        for j in range(n_seg - 1):
            @pl.when(j < seg)
            def _():
                pltpu.make_async_remote_copy(
                    src_ref=transfer_ref.at[0, 0], dst_ref=arrived.at[j],
                    send_sem=t_send.at[0], recv_sem=t_recv.at[j],
                    device_id=(seg - 1, me), device_id_type=MESH,
                ).wait_recv()
                flip(arrived[j])
                left_wide[...] = advance(left_wide[...], arrived[j])

    left_out[0, 0] = left_wide[...].astype(bf16)

    for c in range(CHUNKS):
        cs = pl.ds(c * width, width)
        middle[:, cs] = mm(left_out[0, 0], vec[c].astype(bf16)).astype(bf16)
    block = size // ROW_BLOCKS
    zero = jnp.zeros((1, 128), f32)

    def passes(body, sums_count):
        def one(i, parts):
            found = body(pl.ds(pl.multiple_of(i * block, block), block))
            return tuple(p + folded8(x) for p, x in zip(parts, found))

        start = tuple(jnp.zeros((8, 128), f32) for _ in range(sums_count))
        parts = lax.fori_loop(0, ROW_BLOCKS, one, start)
        return [jnp.sum(p, axis=0, keepdims=True) for p in parts]

    def live_block(c, rows):
        row = lax.broadcasted_iota(jnp.int32, (block, width), 0) + rows.start
        col = lax.broadcasted_iota(jnp.int32, (block, width), 1) + c * width
        return (row < rows_ref[0]) & (col < cols_ref[0])

    def diagonal(step):
        for c in range(CHUNKS):
            cs = pl.ds(c * width, width)
            middle[:, cs] = mm(left_out[0, 0], field[step, c]).astype(bf16)
        for c in range(CHUNKS):
            cs = pl.ds(c * width, width)
            app[c] = mm(middle[...], right_blk[:, cs])

    def hop(step, c):
        take_field(step, c)
        app[c] += mm(coupling[...], prev[step, c]) + mm(lifted_coupling[...], foll[step, c])

    energy_part = zero
    for c in range(CHUNKS):
        cs = pl.ds(c * width, width)
        app[c] += mm(middle[...], right_blk[:, cs])

        def first_pass(rows):
            image = jnp.where(live_block(c, rows), app[c, rows], 0.0)
            img[c, rows] = image
            field[1, c, rows] = image.astype(bf16)
            return (vec[c, rows] * image,)

        (part,) = passes(first_pass, 1)
        energy_part += part
        if c == CHUNKS - 1:
            sum_start(1, [energy_part])
        send_field(1, c)
    diagonal(1)
    (energy,) = sum_finish(1, 1)
    first_out[0] = energy[0, 0]
    level[...] = jnp.broadcast_to(energy, level.shape)

    totals = [zero, zero, zero]
    for c in range(CHUNKS):
        hop(1, c)

        def second_pass(rows):
            twice = jnp.where(live_block(c, rows), app[c, rows], 0.0)
            him[c, rows] = twice
            image = img[c, rows]
            corr = image - energy * vec[c, rows]
            applied = twice - energy * image
            field[2, c, rows] = applied.astype(bf16)
            return corr * corr, image * corr, corr * applied

        totals = [t + p for t, p in zip(totals, passes(second_pass, 3))]
        if c == CHUNKS - 1:
            sum_start(2, totals)
        send_field(2, c)

    def rotate(step):
        energy = level[0:1, 0:1]
        corr_norm, cross_term, curv_term = sum_finish(step + 1, 3)
        scale_norm = jnp.sqrt(corr_norm + epsilon)
        offdiag = cross_term / scale_norm
        diag_value = curv_term / (corr_norm + epsilon)
        half_gap = (diag_value - energy) / 2
        lowest = (energy + diag_value) / 2 - jnp.sqrt(half_gap * half_gap + offdiag * offdiag)
        rotation = lowest - energy
        radius = jnp.sqrt(offdiag * offdiag + rotation * rotation + epsilon)
        level[...] = jnp.broadcast_to(lowest, level.shape)
        return energy, lowest, offdiag / radius, rotation / scale_norm / radius

    def sweep(step, carry):
        diagonal(step + 1)
        energy, lowest, keep, turn = rotate(step)
        stay = keep - turn * energy
        totals = [zero, zero, zero]
        for c in range(CHUNKS):
            hop(step + 1, c)

            def update(rows):
                vector, image, twice = vec[c, rows], img[c, rows], him[c, rows]
                more = jnp.where(live_block(c, rows), app[c, rows], 0.0)
                vector = stay * vector + turn * image
                image = stay * image + turn * twice
                twice = keep * twice + turn * more
                vec[c, rows] = vector
                img[c, rows] = image
                him[c, rows] = twice
                corr = image - lowest * vector
                applied = twice - lowest * image
                field[step + 2, c, rows] = applied.astype(bf16)
                return corr * corr, image * corr, corr * applied

            totals = [t + p for t, p in zip(totals, passes(update, 3))]
            if c == CHUNKS - 1:
                sum_start(step + 2, totals)

            @pl.when(step < DAVIDSON - 1)
            def _():
                send_field(step + 2, c)

            settle_field(step + 1, c)
        sum_settle(step + 1)
        return carry

    lax.fori_loop(1, DAVIDSON, sweep, 0)
    energy, lowest, keep, turn = rotate(DAVIDSON)
    for c in range(CHUNKS):
        cs = pl.ds(c * width, width)

        def last_pass(rows):
            vector = vec[c, rows]
            corr = img[c, rows] - energy * vector
            vec_out[0, 0, rows, cs] = keep * vector + turn * corr
            return ()

        passes(last_pass, 0)
    energy_out[0] = lowest[0, 0]
    sum_settle(DAVIDSON + 1)

    if square:
        @pl.when(seg == 0)
        def _():
            for i in range(4):
                l_copy(i, 0, 1).wait_send()
                l_copy(i, 1, 2).wait_send()
            step_copy(0, 0, 2, True).wait_send()

        @pl.when(seg == 1)
        def _():
            for i in range(4):
                step_copy(i, i, 3, False).wait_send()
            step_copy(0, 4, 0, False).wait_send()

        for here, turns in ((1, (0, 3)), (2, (1, 2))):
            @pl.when(seg == here)
            def _():
                for i in turns:
                    l_copy(i, 0, 3).wait_send()

        @pl.when(seg == 2)
        def _():
            last_copy().wait_send()

        @pl.when(seg == 3)
        def _():
            for i in (1, 2, 3):
                step_copy(i, i, 2, True).wait_send()
    else:
        for d in range(1, n_seg):
            @pl.when(seg + d < n_seg)
            def _():
                t_copy(d).wait_send()
    for c in range(CHUNKS):
        settle_field(0, c)
        settle_field(1, c)

    @pl.when(has_prev)
    def _():
        coupling_copy().wait_send()

    sum_settle(0)
    sum_settle(1)


def on_device(n_seg, n_op, *arrays):
    size = arrays[0].shape[-1]
    width = size // CHUNKS
    vmem = pl.BlockSpec(memory_space=pltpu.VMEM)
    smem = pl.BlockSpec(memory_space=pltpu.SMEM)
    dma = pltpu.SemaphoreType.DMA
    fields = (STEPS, CHUNKS, size, width)
    return pl.pallas_call(
        functools.partial(kernel, n_seg, n_op),
        out_shape=(
            jax.ShapeDtypeStruct((1, 1, size, size), f32),
            jax.ShapeDtypeStruct((1, 1, size, size), bf16),
            jax.ShapeDtypeStruct((1,), f32),
            jax.ShapeDtypeStruct((1,), f32),
        ),
        in_specs=[pl.BlockSpec(memory_space=pltpu.HBM)] * 5 + [smem] * 2,
        out_specs=(vmem, vmem, smem, smem),
        scratch_shapes=[
            pltpu.VMEM((size, size), bf16),
            pltpu.VMEM((size, size), bf16),
            pltpu.VMEM((size, size), bf16),
            pltpu.VMEM((size, size), bf16),
            pltpu.VMEM((size, size), bf16),
            pltpu.VMEM((size, size), bf16),
            pltpu.VMEM((size, size), bf16),
            pltpu.VMEM(fields, bf16),
            pltpu.VMEM(fields, bf16),
            pltpu.VMEM(fields, bf16),
            pltpu.VMEM((size, size), bf16),
            pltpu.VMEM((size, size), bf16),
            pltpu.VMEM((n_seg - 1, size, size), bf16),
            pltpu.VMEM((size, size), f32),
            pltpu.VMEM((size, size), bf16),
            pltpu.VMEM((size, size), bf16),
            pltpu.VMEM((CHUNKS, size, width), f32),
            pltpu.VMEM((CHUNKS, size, width), f32),
            pltpu.VMEM((CHUNKS, size, width), f32),
            pltpu.VMEM((CHUNKS, size, width), f32),
            pltpu.VMEM((ROUNDS, n_op, 8, 128), f32),
            pltpu.VMEM((8, 128), f32),
            dma((5,)),
            dma((2, 4)),
            dma((4,)),
            dma((STEPS, 2, CHUNKS)),
            dma((STEPS, CHUNKS)),
            dma((STEPS, CHUNKS)),
            dma((n_seg + 1,)),
            dma((n_seg + 1,)),
            dma,
            dma,
            dma((ROUNDS, n_op)),
            dma((ROUNDS, n_op)),
        ],
        compiler_params=pltpu.CompilerParams(
            collective_id=0, has_side_effects=True, vmem_limit_bytes=VMEM_LIMIT
        ),
        cost_estimate=pl.CostEstimate(
            flops=2 * 30 * size**3, bytes_accessed=8 * size * size * 2, transcendentals=0
        ),
        name="segment_solve",
    )(*arrays)


def solution(mesh):
    placed = (
        P("seg", "op", None, None),
        P("op", None, None),
        P("seg", "op", None, None),
        P("seg", "op", None, None),
        P("seg", "op", None, None),
        P("op"),
        P("op"),
    )
    return jax.shard_map(
        functools.partial(on_device, mesh.shape["seg"], mesh.shape["op"]),
        mesh=mesh,
        in_specs=placed,
        out_specs=(P("seg", "op", None, None), P("seg", "op", None, None), P("seg"), P("seg")),
        check_vma=False,
    )
```

```python
import functools

import jax
import jax.numpy as jnp
from jax import lax
from jax.experimental import pallas as pl
from jax.experimental.pallas import tpu as pltpu
from jax.sharding import PartitionSpec as P

DAVIDSON = 4
STEPS = DAVIDSON + 2
ROUNDS = DAVIDSON + 2
CHUNKS = 2
ROW_BLOCKS = 16
VMEM_LIMIT = 63 * 1024 * 1024

epsilon = 1e-06

MESH = pl.DeviceIdType.MESH
f32 = jnp.float32
bf16 = jnp.bfloat16


def mm(a, b):
    return jnp.dot(a, b, preferred_element_type=f32)


def split(x):
    high = x.astype(bf16)
    return high, (x - high.astype(f32)).astype(bf16)


def folded8(x):
    rows, width = x.shape
    x = jnp.sum(x.reshape(rows // 8, 8, width), axis=0)
    acc = x[:, :128]
    for start in range(128, width, 128):
        acc = acc + x[:, start : start + 128]
    return acc


def folded(x):
    return jnp.sum(folded8(x), axis=0, keepdims=True)


def kernel(
    n_seg, n_op,
    theta_ref, edge_ref, transfer_ref, right_ref, coupling_ref, rows_ref, cols_ref,
    vec_out, left_out, energy_out, first_out,
    theta, edge, right, coupling, own_step, first_left, flipped,
    field, prev, foll, next_coupling, lifted_coupling, arrived, left_wide, right_blk,
    middle, vec, img, him, app, sums, level,
    load_sem, l_send, l_recv, field_send, prev_recv, foll_recv, t_send, t_recv, c_send, c_recv, sum_send, sum_recv,
):
    seg = lax.axis_index("seg")
    me = lax.axis_index("op")
    size = theta_ref.shape[-1]
    width = size // CHUNKS
    square = n_seg == 4
    has_prev = me > 0
    has_next = me < n_op - 1

    loads = [
        pltpu.make_async_copy(ref, held, load_sem.at[i])
        for i, (ref, held) in enumerate((
            (theta_ref.at[0, 0], theta), (coupling_ref.at[0, 0], coupling),
            (edge_ref.at[0], edge), (transfer_ref.at[0, 0], own_step), (right_ref.at[0, 0], right),
        ))
    ]
    for load in loads:
        load.start()

    barrier = pltpu.get_barrier_semaphore()
    for d in range(1, n_seg):
        pl.semaphore_signal(
            barrier, inc=1, device_id=(lax.rem(seg + d, n_seg), me), device_id_type=MESH
        )
    for d in range(1, n_op):
        pl.semaphore_signal(
            barrier, inc=1, device_id=(seg, lax.rem(me + d, n_op)), device_id_type=MESH
        )

    live_rows = lax.broadcasted_iota(jnp.int32, (size, width), 0) < rows_ref[0]

    def live(c):
        cols = lax.broadcasted_iota(jnp.int32, (size, width), 1) + c * width
        return live_rows & (cols < cols_ref[0])

    loads[0].wait()
    for c in range(CHUNKS):
        cs = pl.ds(c * width, width)
        field[0, c] = jnp.where(live(c), theta[:, cs].astype(f32), 0.0).astype(bf16)

    pl.semaphore_wait(barrier, n_seg + n_op - 2)

    def t_copy(d):
        return pltpu.make_async_remote_copy(
            src_ref=transfer_ref.at[0, 0], dst_ref=arrived.at[seg],
            send_sem=t_send.at[d], recv_sem=t_recv.at[seg],
            device_id=(seg + d, me), device_id_type=MESH,
        )

    quarter = size // 4

    def rows_of(i):
        return pl.ds(i * quarter, quarter)

    def l_copy(i, path, target):
        part = first_left.at[rows_of(i), pl.ds(i * quarter, size - i * quarter)]
        return pltpu.make_async_remote_copy(
            src_ref=part, dst_ref=part, send_sem=l_send.at[path, i], recv_sem=l_recv.at[i],
            device_id=(target, me), device_id_type=MESH,
        )

    def step_copy(i, sem, target, forwarded):
        part = arrived.at[1, rows_of(i)]
        return pltpu.make_async_remote_copy(
            src_ref=part if forwarded else transfer_ref.at[0, 0, rows_of(i)], dst_ref=part,
            send_sem=t_send.at[sem], recv_sem=t_recv.at[i],
            device_id=(target, me), device_id_type=MESH,
        )

    def last_copy():
        return pltpu.make_async_remote_copy(
            src_ref=transfer_ref.at[0, 0], dst_ref=arrived.at[2],
            send_sem=t_send.at[4], recv_sem=t_recv.at[4],
            device_id=(3, me), device_id_type=MESH,
        )

    if square:
        @pl.when(seg == 1)
        def _():
            for i in (1, 2, 3):
                step_copy(i, i, 3, False).start()
            step_copy(0, 4, 0, False).start()
            step_copy(0, 0, 3, False).start()

        @pl.when(seg == 2)
        def _():
            last_copy().start()
    else:
        for d in range(1, n_seg):
            @pl.when(seg + d < n_seg)
            def _():
                t_copy(d).start()

    def up_copy(step, c):
        return pltpu.make_async_remote_copy(
            src_ref=field.at[step, c], dst_ref=prev.at[step, c],
            send_sem=field_send.at[step, 0, c], recv_sem=prev_recv.at[step, c],
            device_id=(seg, me + 1), device_id_type=MESH,
        )

    def down_copy(step, c):
        return pltpu.make_async_remote_copy(
            src_ref=field.at[step, c], dst_ref=foll.at[step, c],
            send_sem=field_send.at[step, 1, c], recv_sem=foll_recv.at[step, c],
            device_id=(seg, me - 1), device_id_type=MESH,
        )

    def send_field(step, c):
        @pl.when(has_next)
        def _():
            up_copy(step, c).start()

        @pl.when(has_prev)
        def _():
            down_copy(step, c).start()

    def take_field(step, c):
        @pl.when(has_prev)
        def _():
            up_copy(step, c).wait_recv()

        @pl.when(has_next)
        def _():
            down_copy(step, c).wait_recv()

    def settle_field(step, c):
        @pl.when(has_next)
        def _():
            up_copy(step, c).wait_send()

        @pl.when(has_prev)
        def _():
            down_copy(step, c).wait_send()

    def coupling_copy():
        return pltpu.make_async_remote_copy(
            src_ref=coupling_ref.at[0, 0], dst_ref=next_coupling,
            send_sem=c_send, recv_sem=c_recv,
            device_id=(seg, me - 1), device_id_type=MESH,
        )

    for c in range(CHUNKS):
        send_field(0, c)

    @pl.when(has_prev)
    def _():
        coupling_copy().start()

    def sum_copy(rnd, d):
        return pltpu.make_async_remote_copy(
            src_ref=sums.at[rnd, me], dst_ref=sums.at[rnd, me],
            send_sem=sum_send.at[rnd, d], recv_sem=sum_recv.at[rnd, me],
            device_id=(seg, lax.rem(me + d, n_op)), device_id_type=MESH,
        )

    def sum_start(rnd, parts):
        row = lax.broadcasted_iota(jnp.int32, (8, 128), 0)
        tile = jnp.zeros((8, 128), f32)
        for i, part in enumerate(parts):
            tile = jnp.where(row == i, part, tile)
        sums[rnd, me] = tile
        for d in range(1, n_op):
            sum_copy(rnd, d).start()

    def sum_finish(rnd, count):
        for d in range(1, n_op):
            source = lax.rem(me + d, n_op)
            pltpu.make_async_remote_copy(
                src_ref=sums.at[rnd, source], dst_ref=sums.at[rnd, source],
                send_sem=sum_send.at[rnd, d], recv_sem=sum_recv.at[rnd, source],
                device_id=(seg, source), device_id_type=MESH,
            ).wait_recv()
        total = sums[rnd, 0]
        for p in range(1, n_op):
            total = total + sums[rnd, p]
        total = jnp.sum(total, axis=1, keepdims=True)
        return [total[i : i + 1] for i in range(count)]

    def sum_settle(rnd):
        for d in range(1, n_op):
            sum_copy(rnd, d).wait_send()

    start_part = jnp.zeros((1, 128), f32)
    for c in range(CHUNKS):
        wide = field[0, c].astype(f32)
        start_part += folded(wide * wide)
    sum_start(0, [start_part])

    for load in loads[1:]:
        load.wait()
    edge_wide = edge[...].astype(f32)
    left_wide[...] = 0.5 * (edge_wide + edge_wide.T)

    def flip(step):
        flipped[...] = step.astype(f32).T.astype(bf16)

    def advance(left, step):
        if left.dtype == bf16:
            image = mm(left, step)
        else:
            high, rest = split(left)
            image = mm(high, step) + mm(rest, step)
        high, rest = split(image)
        return mm(flipped[...], high) + mm(flipped[...], rest)

    def mirror():
        for i in range(4):
            for j in range(i + 1, 4):
                block = first_left[rows_of(i), rows_of(j)].astype(f32)
                first_left[rows_of(j), rows_of(i)] = block.T.astype(bf16)

    if square:
        @pl.when(seg == 0)
        def _():
            flip(own_step[...])
            first_left[...] = advance(left_wide[...], own_step[...]).astype(bf16)
            for i in range(4):
                l_copy(i, 0, 1).start()
                l_copy(i, 1, 2).start()
            step_copy(0, 0, 2, True).wait_recv()
            step_copy(0, 0, 2, True).start()

        for here, turns in ((1, (0, 3)), (2, (1, 2))):
            @pl.when(seg == here)
            def _():
                for i in turns:
                    l_copy(i, 0, 3).wait_recv()
                    l_copy(i, 0, 3).start()

        @pl.when(seg == 3)
        def _():
            for i in (1, 2, 3):
                step_copy(i, i, 2, True).wait_recv()
                step_copy(i, i, 2, True).start()

    right_wide = right[...].astype(f32)
    right_blk[...] = (0.5 * (right_wide + right_wide.T)).astype(bf16)

    @pl.when(jnp.logical_not(has_prev))
    def _():
        prev[...] = jnp.zeros_like(prev)

    @pl.when(jnp.logical_not(has_next))
    def _():
        foll[...] = jnp.zeros_like(foll)
        lifted_coupling[...] = jnp.zeros_like(lifted_coupling)

    (start_total,) = sum_finish(0, 1)
    start_norm = jnp.sqrt(start_total + epsilon)

    @pl.when(has_next)
    def _():
        down = coupling_copy()
        down.wait_recv()
        lifted_coupling[...] = next_coupling[...].astype(f32).T.astype(bf16)

    for c in range(CHUNKS):
        vec[c] = field[0, c].astype(f32) / start_norm
        take_field(0, c)
        before = (prev[0, c].astype(f32) / start_norm).astype(bf16)
        after = (foll[0, c].astype(f32) / start_norm).astype(bf16)
        app[c] = mm(coupling[...], before) + mm(lifted_coupling[...], after)

    if square:
        @pl.when(seg == 1)
        def _():
            for i in (1, 2):
                l_copy(i, 0, 3).wait_recv()
            mirror()
            left_wide[...] = first_left[...].astype(f32)

        @pl.when(seg == 2)
        def _():
            for i in range(4):
                step_copy(i, 0, 3, True).wait_recv()
            flip(arrived[1])
            for i in (0, 3):
                l_copy(i, 0, 3).wait_recv()
            mirror()
            left_wide[...] = advance(first_left[...], arrived[1])

        @pl.when(seg == 3)
        def _():
            step_copy(0, 0, 2, True).wait_recv()
            flip(arrived[1])
            for i in range(4):
                l_copy(i, 0, 3).wait_recv()
            mirror()
            left_wide[...] = advance(first_left[...], arrived[1])
            last_copy().wait_recv()
            flip(arrived[2])
            left_wide[...] = advance(left_wide[...], arrived[2])
    else:
        for j in range(n_seg - 1):
            @pl.when(j < seg)
            def _():
                pltpu.make_async_remote_copy(
                    src_ref=transfer_ref.at[0, 0], dst_ref=arrived.at[j],
                    send_sem=t_send.at[0], recv_sem=t_recv.at[j],
                    device_id=(seg - 1, me), device_id_type=MESH,
                ).wait_recv()
                flip(arrived[j])
                left_wide[...] = advance(left_wide[...], arrived[j])

    left_out[0, 0] = left_wide[...].astype(bf16)

    for c in range(CHUNKS):
        cs = pl.ds(c * width, width)
        middle[:, cs] = mm(left_out[0, 0], vec[c].astype(bf16)).astype(bf16)
    block = size // ROW_BLOCKS
    zero = jnp.zeros((1, 128), f32)

    def passes(body, sums_count):
        def one(i, parts):
            found = body(pl.ds(pl.multiple_of(i * block, block), block))
            return tuple(p + folded8(x) for p, x in zip(parts, found))

        start = tuple(jnp.zeros((8, 128), f32) for _ in range(sums_count))
        parts = lax.fori_loop(0, ROW_BLOCKS, one, start, unroll=4)
        return [jnp.sum(p, axis=0, keepdims=True) for p in parts]

    def live_block(c, rows):
        row = lax.broadcasted_iota(jnp.int32, (block, width), 0) + rows.start
        col = lax.broadcasted_iota(jnp.int32, (block, width), 1) + c * width
        return (row < rows_ref[0]) & (col < cols_ref[0])

    def diagonal(step):
        for c in range(CHUNKS):
            cs = pl.ds(c * width, width)
            middle[:, cs] = mm(left_out[0, 0], field[step, c]).astype(bf16)
        for c in range(CHUNKS):
            cs = pl.ds(c * width, width)
            app[c] = mm(middle[...], right_blk[:, cs])

    def hop(step, c):
        take_field(step, c)
        app[c] += mm(coupling[...], prev[step, c]) + mm(lifted_coupling[...], foll[step, c])

    energy_part = zero
    for c in range(CHUNKS):
        cs = pl.ds(c * width, width)
        app[c] += mm(middle[...], right_blk[:, cs])

        def first_pass(rows):
            image = jnp.where(live_block(c, rows), app[c, rows], 0.0)
            img[c, rows] = image
            field[1, c, rows] = image.astype(bf16)
            return (vec[c, rows] * image,)

        (part,) = passes(first_pass, 1)
        energy_part += part
        if c == CHUNKS - 1:
            sum_start(1, [energy_part])
        send_field(1, c)
    diagonal(1)
    (energy,) = sum_finish(1, 1)
    first_out[0] = energy[0, 0]
    level[...] = jnp.broadcast_to(energy, level.shape)

    totals = [zero, zero, zero]
    for c in range(CHUNKS):
        hop(1, c)

        def second_pass(rows):
            twice = jnp.where(live_block(c, rows), app[c, rows], 0.0)
            him[c, rows] = twice
            image = img[c, rows]
            corr = image - energy * vec[c, rows]
            applied = twice - energy * image
            field[2, c, rows] = applied.astype(bf16)
            return corr * corr, image * corr, corr * applied

        totals = [t + p for t, p in zip(totals, passes(second_pass, 3))]
        if c == CHUNKS - 1:
            sum_start(2, totals)
        send_field(2, c)

    def rotate(step):
        energy = level[0:1, 0:1]
        corr_norm, cross_term, curv_term = sum_finish(step + 1, 3)
        scale_norm = jnp.sqrt(corr_norm + epsilon)
        offdiag = cross_term / scale_norm
        diag_value = curv_term / (corr_norm + epsilon)
        half_gap = (diag_value - energy) / 2
        lowest = (energy + diag_value) / 2 - jnp.sqrt(half_gap * half_gap + offdiag * offdiag)
        rotation = lowest - energy
        radius = jnp.sqrt(offdiag * offdiag + rotation * rotation + epsilon)
        level[...] = jnp.broadcast_to(lowest, level.shape)
        return energy, lowest, offdiag / radius, rotation / scale_norm / radius

    def sweep(step, carry):
        diagonal(step + 1)
        energy, lowest, keep, turn = rotate(step)
        stay = keep - turn * energy
        totals = [zero, zero, zero]
        for c in range(CHUNKS):
            hop(step + 1, c)

            def update(rows):
                vector, image, twice = vec[c, rows], img[c, rows], him[c, rows]
                more = jnp.where(live_block(c, rows), app[c, rows], 0.0)
                vector = stay * vector + turn * image
                image = stay * image + turn * twice
                twice = keep * twice + turn * more
                vec[c, rows] = vector
                img[c, rows] = image
                him[c, rows] = twice
                corr = image - lowest * vector
                applied = twice - lowest * image
                field[step + 2, c, rows] = applied.astype(bf16)
                return corr * corr, image * corr, corr * applied

            totals = [t + p for t, p in zip(totals, passes(update, 3))]
            if c == CHUNKS - 1:
                sum_start(step + 2, totals)

            @pl.when(step < DAVIDSON - 1)
            def _():
                send_field(step + 2, c)

            settle_field(step + 1, c)
        sum_settle(step + 1)
        return carry

    lax.fori_loop(1, DAVIDSON, sweep, 0)
    energy, lowest, keep, turn = rotate(DAVIDSON)
    for c in range(CHUNKS):
        cs = pl.ds(c * width, width)

        def last_pass(rows):
            vector = vec[c, rows]
            corr = img[c, rows] - energy * vector
            vec_out[0, 0, rows, cs] = keep * vector + turn * corr
            return ()

        passes(last_pass, 0)
    energy_out[0] = lowest[0, 0]
    sum_settle(DAVIDSON + 1)

    if square:
        @pl.when(seg == 0)
        def _():
            for i in range(4):
                l_copy(i, 0, 1).wait_send()
                l_copy(i, 1, 2).wait_send()
            step_copy(0, 0, 2, True).wait_send()

        @pl.when(seg == 1)
        def _():
            for i in range(4):
                step_copy(i, i, 3, False).wait_send()
            step_copy(0, 4, 0, False).wait_send()

        for here, turns in ((1, (0, 3)), (2, (1, 2))):
            @pl.when(seg == here)
            def _():
                for i in turns:
                    l_copy(i, 0, 3).wait_send()

        @pl.when(seg == 2)
        def _():
            last_copy().wait_send()

        @pl.when(seg == 3)
        def _():
            for i in (1, 2, 3):
                step_copy(i, i, 2, True).wait_send()
    else:
        for d in range(1, n_seg):
            @pl.when(seg + d < n_seg)
            def _():
                t_copy(d).wait_send()
    for c in range(CHUNKS):
        settle_field(0, c)
        settle_field(1, c)

    @pl.when(has_prev)
    def _():
        coupling_copy().wait_send()

    sum_settle(0)
    sum_settle(1)


def on_device(n_seg, n_op, *arrays):
    size = arrays[0].shape[-1]
    width = size // CHUNKS
    vmem = pl.BlockSpec(memory_space=pltpu.VMEM)
    smem = pl.BlockSpec(memory_space=pltpu.SMEM)
    dma = pltpu.SemaphoreType.DMA
    fields = (STEPS, CHUNKS, size, width)
    return pl.pallas_call(
        functools.partial(kernel, n_seg, n_op),
        out_shape=(
            jax.ShapeDtypeStruct((1, 1, size, size), f32),
            jax.ShapeDtypeStruct((1, 1, size, size), bf16),
            jax.ShapeDtypeStruct((1,), f32),
            jax.ShapeDtypeStruct((1,), f32),
        ),
        in_specs=[pl.BlockSpec(memory_space=pltpu.HBM)] * 5 + [smem] * 2,
        out_specs=(vmem, vmem, smem, smem),
        scratch_shapes=[
            pltpu.VMEM((size, size), bf16),
            pltpu.VMEM((size, size), bf16),
            pltpu.VMEM((size, size), bf16),
            pltpu.VMEM((size, size), bf16),
            pltpu.VMEM((size, size), bf16),
            pltpu.VMEM((size, size), bf16),
            pltpu.VMEM((size, size), bf16),
            pltpu.VMEM(fields, bf16),
            pltpu.VMEM(fields, bf16),
            pltpu.VMEM(fields, bf16),
            pltpu.VMEM((size, size), bf16),
            pltpu.VMEM((size, size), bf16),
            pltpu.VMEM((n_seg - 1, size, size), bf16),
            pltpu.VMEM((size, size), f32),
            pltpu.VMEM((size, size), bf16),
            pltpu.VMEM((size, size), bf16),
            pltpu.VMEM((CHUNKS, size, width), f32),
            pltpu.VMEM((CHUNKS, size, width), f32),
            pltpu.VMEM((CHUNKS, size, width), f32),
            pltpu.VMEM((CHUNKS, size, width), f32),
            pltpu.VMEM((ROUNDS, n_op, 8, 128), f32),
            pltpu.VMEM((8, 128), f32),
            dma((5,)),
            dma((2, 4)),
            dma((4,)),
            dma((STEPS, 2, CHUNKS)),
            dma((STEPS, CHUNKS)),
            dma((STEPS, CHUNKS)),
            dma((n_seg + 1,)),
            dma((n_seg + 1,)),
            dma,
            dma,
            dma((ROUNDS, n_op)),
            dma((ROUNDS, n_op)),
        ],
        compiler_params=pltpu.CompilerParams(
            collective_id=0, has_side_effects=True, vmem_limit_bytes=VMEM_LIMIT
        ),
        cost_estimate=pl.CostEstimate(
            flops=2 * 30 * size**3, bytes_accessed=8 * size * size * 2, transcendentals=0
        ),
        name="segment_solve",
    )(*arrays)


def solution(mesh):
    placed = (
        P("seg", "op", None, None),
        P("op", None, None),
        P("seg", "op", None, None),
        P("seg", "op", None, None),
        P("seg", "op", None, None),
        P("op"),
        P("op"),
    )
    return jax.shard_map(
        functools.partial(on_device, mesh.shape["seg"], mesh.shape["op"]),
        mesh=mesh,
        in_specs=placed,
        out_specs=(P("seg", "op", None, None), P("seg", "op", None, None), P("seg"), P("seg")),
        check_vma=False,
    )
```
